32 devices in a mesh: node: 4 (over z), dev: 8 (over y, x, core).
Axes of the slice: x: 2, y: 2, z: 4, core: 2. Of those that a mesh axis runs over, the one named last changes fastest.
Arguments:
- amps: float32 [4, 8, 8, 1024], P('node', 'dev'), may hold values from -6 to 6
- amp_tile: int32 [4, 8], replicated, may hold values from 0 to 7, each once within a row
- ints: float32 [4, 8, 1024, 1024], P('node', 'dev'), may hold values from -0.1875 to 0.1875
- tasks: int32 [4, 16, 2], replicated, may hold values from 0 to 7, as said below
- pair_energy: float32 [4, 8], P('node', 'dev'), may hold values from -3 to -1
- virt_energy: float32 [4, 1024], replicated, may hold values from 0.5 to 3
Outputs:
- resid: float32 [4, 8, 4096], P('node', 'dev')
The draws below stay inside these ranges and needn't reach their ends.
Inputs may be any that keep to these rules, and one draw needn't show every extreme that they name: Each row amp_tile[n] is a permutation of the 8 contracted tile pairs. `tasks`: the first column names an output tile pair below 4, the second a contracted tile pair below 8; the (ab, cd) pairs of one pair block are distinct.
All inputs are finite; a program needn't handle non-finite values.
Results may differ from the reference program's by a relative error of at most 0.0003.
Values sent between devices are 32-bit elements; how exact they have to be, the bound alone decides.
No kernel may reach another device: no remote copies, remote signals or barrier semaphores. Data moves between devices by JAX's collectives and lax.ppermute only.
A program may use at most 64 MiB of HBM per device.

```python
import jax
import jax.numpy as jnp
from jax import lax

TT = 1024
P_SIZE = 8
NVT = 8
NAB = 4
NIJ = 4
NTASK = 16


def draw_tasks(key, part):
    key_level, key_noise = jax.random.split(jax.random.fold_in(key, 7))
    level = jax.random.randint(key_level, (NIJ, NVT), 0, 4)
    noise = jax.random.randint(key_noise, (NIJ, NAB * NVT), 0, 2048)
    index = jnp.arange(NAB * NVT, dtype=jnp.int32)
    weight = jnp.take(level, index % NVT, axis=1)
    score = (noise + weight * 1024) * (NAB * NVT) + index[None, :]
    order = jnp.argsort(-score, axis=1)
    chosen = order[:, :NTASK]
    return jnp.stack([chosen // NVT, chosen % NVT], axis=-1).astype(jnp.int32)


def shard_levels(stream_key, dims, shards, least, high):
    def one(position, parts):
        steps = jax.random.uniform(jax.random.fold_in(jax.random.fold_in(stream_key, 6), position), (parts,), jnp.float32, least / len(shards), high / len(shards))
        return jnp.repeat(jnp.exp(steps), dims[position] // parts).reshape((-1,) + (1,) * (len(dims) - position - 1))

    level = one(*shards[0])
    for cut in shards[1:]:
        level = level * one(*cut)
    return level


def normal_values(rng, dims, deviation, reach, shards=(), kind=jnp.bfloat16):
    array = jax.random.normal(rng, dims, jnp.float32) * deviation
    if len(shards) > 0:
        array = shard_levels(rng, dims, shards, -0.22, 0.18) * array
    return jnp.clip(array, min=-reach, max=reach).astype(kind)


def setup_inputs(seed: int = 0) -> dict:
    streams_of = jax.random.split(jax.random.key(seed), 7)
    amps = normal_values(streams_of[0], (NIJ, NVT, P_SIZE, TT), 1.0, 6.0, ((0, 4), (1, 8)), jnp.float32)
    amp_tile = jax.vmap(lambda own: jax.random.permutation(own, NVT))(jax.random.split(streams_of[1], NIJ)).reshape((NIJ, NVT)).astype(jnp.int32)
    ints = normal_values(streams_of[2], (NAB, NVT, TT, TT), TT ** -0.5, 0.1875, ((0, 4), (1, 8)), jnp.float32)
    tasks = draw_tasks(jax.random.fold_in(streams_of[6], 71), 0)
    pair_energy = jnp.clip(-3.0 + 2.0 * jax.random.uniform(streams_of[4], (NIJ, P_SIZE), jnp.float32) ** shard_levels(streams_of[4], (NIJ, P_SIZE), ((0, 4), (1, 8)), -0.2, 0.2), -3.0, -1.0)
    virt_energy = jnp.clip(jax.random.uniform(streams_of[5], (NAB, TT), jnp.float32, 0.5, 3.0), 0.5, 3.0)
    return dict(amps=amps, amp_tile=amp_tile, ints=ints, tasks=tasks, pair_energy=pair_energy, virt_energy=virt_energy)


def tile_product(left, right):
    return lax.dot_general(left, right, (((1,), (1,)), ((), ())), precision=lax.Precision.HIGHEST, preferred_element_type=jnp.float32)


def reference(amps, amp_tile, ints, tasks, pair_energy, virt_energy):
    width = amps.shape[3]
    pairs = amps.shape[2]
    count = amps.shape[1]
    out_count = ints.shape[0]

    def row_work(block):
        slots = amp_tile[block]
        inverse = jnp.zeros((count,), jnp.int32).at[slots].set(jnp.arange(count, dtype=jnp.int32))
        ordered = amps[block][inverse]

        def task_step(ladder, task):
            ab_tile = task[0].astype(jnp.int32)
            cd_tile = task[1].astype(jnp.int32)
            product = tile_product(ordered[cd_tile], ints[ab_tile, cd_tile])
            offset = (ab_tile * width).astype(jnp.int32)
            current = lax.dynamic_slice_in_dim(ladder, offset, width, 1)
            return lax.dynamic_update_slice_in_dim(ladder, current + product, offset, 1), None

        ladder, _ = lax.scan(task_step, jnp.zeros((pairs, out_count * width), jnp.float32), tasks[block])
        return ladder

    ladder = lax.map(row_work, jnp.arange(amps.shape[0], dtype=jnp.int32))
    denominator = pair_energy[:, :, None] - virt_energy.reshape(1, 1, -1)
    return ladder / denominator
```

```python
import jax
import jax.numpy as jnp
from jax import lax
from jax.sharding import PartitionSpec as P


def on_device(amps, amp_tile, ints, tasks, pair_energy, virt_energy):
    nodes, devs = lax.axis_size("node"), lax.axis_size("dev")
    my_node, my_dev = lax.axis_index("node"), lax.axis_index("dev")
    pairs, width = amps.shape[2], amps.shape[3]

    slots = lax.all_gather(amps[0, 0], "dev", axis=0)
    wanted = lax.dynamic_index_in_dim(amp_tile, my_node, 0, keepdims=False) == my_dev
    mine = jnp.sum(jnp.where(wanted[:, None, None], slots, 0.0), axis=0)

    arrived = [mine] + [
        lax.ppermute(mine, "node", [(i, i ^ k) for i in range(nodes)])
        for k in range(1, nodes)
    ]
    blocks = my_node ^ jnp.arange(nodes, dtype=jnp.int32)
    hit = jnp.any((tasks[:, :, 0] == my_node) & (tasks[:, :, 1] == my_dev), axis=1)
    stacked = jnp.stack(arrived)
    ordered = jnp.stack(
        [lax.dynamic_index_in_dim(stacked, blocks[k], 0, keepdims=False) for k in range(nodes)]
    )
    ordered = jnp.where(hit[:, None, None], ordered, 0.0)
    products = lax.dot_general(
        ordered.reshape(nodes * pairs, width),
        ints[0, 0],
        (((1,), (1,)), ((), ())),
        precision=lax.Precision.HIGH,
        preferred_element_type=jnp.float32,
    )

    terms = lax.all_to_all(products, ("node", "dev"), 0, 0, tiled=True)
    ladder = jnp.sum(terms.reshape(nodes, devs, width), axis=1)
    resid = ladder / (pair_energy - virt_energy)
    return resid.reshape(1, 1, nodes * width)


def solution(mesh):
    in_specs = (
        P("node", "dev", None, None),
        P(),
        P("node", "dev", None, None),
        P(),
        P("node", "dev"),
        P(),
    )
    return jax.shard_map(
        on_device, mesh=mesh, in_specs=in_specs, out_specs=P("node", "dev", None), check_vma=False
    )
```

```python
import jax
import jax.numpy as jnp
from jax import lax
from jax.experimental import pallas as pl
from jax.experimental.pallas import tpu as pltpu
from jax.sharding import PartitionSpec as P

LANES = 128
VMEM_LIMIT = 24 * 2**20
CONTRACT_LAST = (((1,), (1,)), ((), ()))
MINE, THEIRS, HITS = 0, 1, 2
VMEM = pl.BlockSpec(memory_space=pltpu.VMEM)
HBM = pl.BlockSpec(memory_space=pltpu.HBM)
CHUNKS = 2


def call(kernel, name, out_shape, in_specs, scratch=(), flops=0, moved=0):
    return pl.pallas_call(
        kernel,
        out_shape=out_shape,
        in_specs=in_specs,
        out_specs=jax.tree.map(lambda _: VMEM, out_shape),
        scratch_shapes=list(scratch),
        compiler_params=pltpu.CompilerParams(vmem_limit_bytes=VMEM_LIMIT),
        cost_estimate=pl.CostEstimate(flops=flops, bytes_accessed=moved, transcendentals=0),
        name=name,
    )


def high_and_low(x):
    high = x.astype(jnp.bfloat16)
    return high, (x - high.astype(jnp.float32)).astype(jnp.bfloat16)


def split_rows(ints_hbm, first, land_ref, sems, high_ref, low_ref):
    chunks = sems.shape[0]
    rows = high_ref.shape[0] // chunks
    copies = [
        pltpu.make_async_copy(
            ints_hbm.at[pl.ds(first + i * rows, rows)], land_ref.at[pl.ds(i * rows, rows)], sems.at[i]
        )
        for i in range(chunks)
    ]
    for copy in copies:
        copy.start()

    def finish():
        for i, copy in enumerate(copies):
            copy.wait()
            part = pl.ds(i * rows, rows)
            high_ref[part, :], low_ref[part, :] = high_and_low(land_ref[part, :])

    return finish


def in_hbm(x):
    return pltpu.with_memory_space_constraint(x, pltpu.HBM)


def stage_kernel(
    tile_hbm, tasks_hbm, amps_hbm, ints_hbm,
    facts_ref, own_ref, high_ref, low_ref,
    tile_ref, tasks_ref, sems, land_ref, ints_sems,
):
    copies = [
        pltpu.make_async_copy(src, dst, sems.at[i])
        for i, (src, dst) in enumerate(
            [(tile_hbm, tile_ref), (tasks_hbm, tasks_ref), (amps_hbm, own_ref)]
        )
    ]
    for copy in copies:
        copy.start()
    finish = split_rows(ints_hbm, 0, land_ref, ints_sems, high_ref, low_ref)
    my_node, my_dev = lax.axis_index("node"), lax.axis_index("dev")
    nodes = tasks_ref.shape[0]
    for copy in copies:
        copy.wait()
    row = tile_ref[pl.ds(my_node, 1), :]
    position = lax.broadcasted_iota(jnp.int32, row.shape, 1)
    for where, owner in ((MINE, my_dev), (THEIRS, my_dev ^ 1)):
        slot = jnp.sum(jnp.where(row == owner, position, 0), axis=1, keepdims=True)
        facts_ref[where : where + 1, :] = jnp.broadcast_to(slot, (1, LANES))
    for k in range(nodes):
        task = tasks_ref[my_node ^ k]
        hit = jnp.where((task[0:1] == my_node) & (task[1:2] == my_dev), 1, 0)
        hit = jnp.max(hit, axis=1, keepdims=True)
        facts_ref[HITS + k : HITS + k + 1, :] = jnp.broadcast_to(hit, (1, LANES))
    finish()


def split_kernel(
    after_ref, pair_ref, virt_hbm, ints_hbm, denom_ref, high_ref, low_ref, virt_ref, sem, land_ref, ints_sems
):
    del after_ref
    copy = pltpu.make_async_copy(virt_hbm, virt_ref, sem)
    copy.start()
    finish = split_rows(
        ints_hbm, ints_hbm.shape[0] - high_ref.shape[0], land_ref, ints_sems, high_ref, low_ref
    )
    copy.wait()
    denom = pair_ref[0, 0] - virt_ref[...]
    for j in range(denom_ref.shape[1]):
        denom_ref[:, j, :] = denom[:, j * LANES : (j + 1) * LANES]
    finish()


def pick_kernel(facts_ref, *refs):
    pieces, (keep_ref, give_ref) = refs[:-2], refs[-2:]
    chip = lax.axis_index("dev") // 2
    for row, out_ref in ((MINE, keep_ref), (THEIRS, give_ref)):
        step = (facts_ref[row : row + 1, 0:1] // 2) ^ chip
        tile = pieces[0][...]
        for j, piece in enumerate(pieces[1:], 1):
            tile = jnp.where(step == j, piece[...], tile)
        out_ref[...] = tile


def merge_kernel(facts_ref, keep_ref, got_ref, mine_ref):
    core = lax.axis_index("dev") % 2
    mine_ref[...] = jnp.where(
        facts_ref[MINE : MINE + 1, 0:1] % 2 == core, keep_ref[...], got_ref[...]
    )


def product_kernel(facts_ref, high_a_ref, low_a_ref, high_b_ref, low_b_ref, *refs):
    pieces, out_ref, rows_ref = refs[:-2], refs[-2], refs[-1]
    my_node = lax.axis_index("node")
    pairs = pieces[0].shape[0]
    total = len(pieces) * pairs
    for k, piece in enumerate(pieces):
        start = pl.multiple_of((my_node ^ k) * pairs, pairs)
        hit = facts_ref[HITS + k : HITS + k + 1, 0:1]
        rows_ref[pl.ds(start, pairs), :] = jnp.where(hit > 0, piece[...], 0.0)
    amp_high, amp_low = high_and_low(rows_ref[...])
    amp_both = jnp.concatenate([amp_high, amp_low], axis=0)
    first = 0
    for high_ref, low_ref in ((high_a_ref, low_a_ref), (high_b_ref, low_b_ref)):
        both = lax.dot_general(
            amp_both, high_ref[...], CONTRACT_LAST, preferred_element_type=jnp.float32
        )
        rest = lax.dot_general(
            amp_high, low_ref[...], CONTRACT_LAST, preferred_element_type=jnp.float32
        )
        result = both[:total] + (both[total:] + rest)
        for j in range(high_ref.shape[0] // LANES):
            out_ref[:, first + j, :] = result[:, j * LANES : (j + 1) * LANES]
        first += high_ref.shape[0] // LANES


def on_device(amps, amp_tile, ints, tasks, pair_energy, virt_energy):
    nodes, devs = lax.axis_size("node"), lax.axis_size("dev")
    pairs, width = amps.shape[2], amps.shape[3]
    groups = width // LANES
    tile = jax.ShapeDtypeStruct((pairs, width), jnp.float32)
    task_rows = jnp.swapaxes(tasks, 1, 2)

    own = amps[0, 0]
    others = [
        lax.ppermute(own, "dev", [(i, i ^ k) for i in range(devs)]) for k in range(2, devs, 2)
    ]
    half = jax.ShapeDtypeStruct((width // 2, width), jnp.bfloat16)
    landing = [pltpu.VMEM(half.shape, jnp.float32), pltpu.SemaphoreType.DMA((CHUNKS,))]
    facts, own, high_a, low_a = call(
        stage_kernel,
        "stage",
        (
            jax.ShapeDtypeStruct((HITS + nodes, LANES), jnp.int32),
            tile,
            half,
            half,
        ),
        [HBM] * 4,
        [
            pltpu.VMEM(amp_tile.shape, jnp.int32),
            pltpu.VMEM(task_rows.shape, jnp.int32),
            pltpu.SemaphoreType.DMA((3,)),
            *landing,
        ],
        flops=width * width,
        moved=4 * width * width,
    )(*map(in_hbm, (amp_tile, task_rows, own, ints[0, 0])))
    slots = [own, *others]
    keep, give = call(pick_kernel, "pick", (tile, tile), [VMEM] * (1 + len(slots)))(facts, *slots)
    got = lax.ppermute(give, "dev", [(i, i ^ 1) for i in range(devs)])
    mine = call(merge_kernel, "merge", tile, [VMEM] * 3)(facts, keep, got)

    pieces = [mine] + [
        lax.ppermute(mine, "node", [(i, i ^ k) for i in range(nodes)])
        for k in range(1, nodes)
    ]
    denom, high_b, low_b = call(
        split_kernel,
        "split",
        (jax.ShapeDtypeStruct((nodes, groups, LANES), jnp.float32), half, half),
        [VMEM, pl.BlockSpec(memory_space=pltpu.SMEM), HBM, HBM],
        [pltpu.VMEM(virt_energy.shape, jnp.float32), pltpu.SemaphoreType.DMA, *landing],
        flops=width * width,
        moved=4 * width * width,
    )(mine, pair_energy, in_hbm(virt_energy), in_hbm(ints[0, 0]))
    products = call(
        product_kernel,
        "product",
        jax.ShapeDtypeStruct((nodes * pairs, groups, LANES), jnp.float32),
        [VMEM] * (5 + nodes),
        [pltpu.VMEM((nodes * pairs, width), jnp.float32)],
        flops=6 * nodes * pairs * width * width,
        moved=4 * width * width,
    )(facts, high_a, low_a, high_b, low_b, *pieces)

    terms = lax.all_to_all(products, ("node", "dev"), 0, 0, tiled=True)
    ladder = jnp.sum(terms.reshape(nodes, devs, groups, LANES), axis=1)
    return (ladder / denom).reshape(1, 1, nodes * width)


def solution(mesh):
    in_specs = (
        P("node", "dev", None, None),
        P(),
        P("node", "dev", None, None),
        P(),
        P("node", "dev"),
        P(),
    )
    return jax.shard_map(
        on_device, mesh=mesh, in_specs=in_specs, out_specs=P("node", "dev", None), check_vma=False
    )
```

```python
import jax
import jax.numpy as jnp
from jax import lax
from jax.experimental import pallas as pl
from jax.experimental.pallas import tpu as pltpu
from jax.sharding import PartitionSpec as P

LANES = 128
VMEM_LIMIT = 24 * 2**20
CONTRACT_LAST = (((1,), (1,)), ((), ()))
HITS = 2
VMEM = pl.BlockSpec(memory_space=pltpu.VMEM)
HBM = pl.BlockSpec(memory_space=pltpu.HBM)
CHUNKS = 2


def call(kernel, name, out_shape, in_specs, scratch=(), flops=0, moved=0):
    return pl.pallas_call(
        kernel,
        out_shape=out_shape,
        in_specs=in_specs,
        out_specs=jax.tree.map(lambda _: VMEM, out_shape),
        scratch_shapes=list(scratch),
        compiler_params=pltpu.CompilerParams(vmem_limit_bytes=VMEM_LIMIT),
        cost_estimate=pl.CostEstimate(flops=flops, bytes_accessed=moved, transcendentals=0),
        name=name,
    )


def high_and_low(x):
    high = x.astype(jnp.bfloat16)
    return high, (x - high.astype(jnp.float32)).astype(jnp.bfloat16)


def split_rows(ints_hbm, first, land_ref, sems, high_ref, low_ref):
    chunks = sems.shape[0]
    rows = high_ref.shape[0] // chunks
    copies = [
        pltpu.make_async_copy(
            ints_hbm.at[pl.ds(first + i * rows, rows)], land_ref.at[pl.ds(i * rows, rows)], sems.at[i]
        )
        for i in range(chunks)
    ]
    for copy in copies:
        copy.start()

    def finish():
        for i, copy in enumerate(copies):
            copy.wait()
            part = pl.ds(i * rows, rows)
            high_ref[part, :], low_ref[part, :] = high_and_low(land_ref[part, :])

    return finish


def in_hbm(x):
    return pltpu.with_memory_space_constraint(x, pltpu.HBM)


def stage_kernel(
    pair_ref, tile_hbm, tasks_hbm, virt_hbm, amps_hbm, ints_hbm,
    facts_ref, denom_ref, own_ref, high_ref, low_ref,
    tile_ref, tasks_ref, virt_ref, sems, land_ref, ints_sems,
):
    copies = [
        pltpu.make_async_copy(src, dst, sems.at[i])
        for i, (src, dst) in enumerate(
            [
                (tile_hbm, tile_ref),
                (tasks_hbm, tasks_ref),
                (virt_hbm, virt_ref),
                (amps_hbm, own_ref),
            ]
        )
    ]
    for copy in copies:
        copy.start()
    finish = split_rows(ints_hbm, 0, land_ref, ints_sems, high_ref, low_ref)
    my_node, my_dev = lax.axis_index("node"), lax.axis_index("dev")
    nodes = tasks_ref.shape[0]
    for copy in copies:
        copy.wait()
    row = tile_ref[pl.ds(my_node, 1), :]
    position = lax.broadcasted_iota(jnp.int32, row.shape, 1)
    for core in range(2):
        owner = my_dev // 2 * 2 + core
        slot = jnp.sum(jnp.where(row == owner, position, 0), axis=1, keepdims=True)
        facts_ref[core : core + 1, :] = jnp.broadcast_to(slot, (1, LANES))
    for k in range(nodes):
        task = tasks_ref[my_node ^ k]
        hit = jnp.where((task[0:1] == my_node) & (task[1:2] == my_dev), 1, 0)
        hit = jnp.max(hit, axis=1, keepdims=True)
        facts_ref[HITS + k : HITS + k + 1, :] = jnp.broadcast_to(hit, (1, LANES))
    denom = pair_ref[0, 0] - virt_ref[...]
    for j in range(denom_ref.shape[1]):
        denom_ref[:, j, :] = denom[:, j * LANES : (j + 1) * LANES]
    finish()


def split_kernel(after_ref, ints_hbm, high_ref, low_ref, land_ref, sems):
    del after_ref
    split_rows(ints_hbm, ints_hbm.shape[0] - high_ref.shape[0], land_ref, sems, high_ref, low_ref)()


def pick_kernel(facts_ref, *refs):
    pieces, held_ref = refs[:-1], refs[-1]
    chip = lax.axis_index("dev") // 2
    for core in range(2):
        step = (facts_ref[core : core + 1, 0:1] // 2) ^ chip
        tile = pieces[0][...]
        for j, piece in enumerate(pieces[1:], 1):
            tile = jnp.where(step == j, piece[...], tile)
        held_ref[core] = tile


def merge_kernel(facts_ref, held_ref, got_ref, both_ref, mine_ref):
    my_core = lax.axis_index("dev") % 2
    for core in range(2):
        here = facts_ref[core : core + 1, 0:1] % 2 == my_core
        both_ref[core] = jnp.where(here, held_ref[core], got_ref[core])
    mine_ref[...] = both_ref[my_core]


def theirs_kernel(after_ref, both_ref, theirs_ref):
    del after_ref
    theirs_ref[...] = both_ref[1 - lax.axis_index("dev") % 2]


def product_kernel(facts_ref, high_a_ref, low_a_ref, high_b_ref, low_b_ref, mine_ref, last_ref, *refs):
    fetched, handed = refs[: len(refs) // 2 - 1], refs[len(refs) // 2 - 1 : -2]
    out_ref, rows_ref = refs[-2:]
    my_node, my_core = lax.axis_index("node"), lax.axis_index("dev") % 2
    pairs = mine_ref.shape[0]
    total = rows_ref.shape[0]

    def place(k, tile):
        start = pl.multiple_of((my_node ^ k) * pairs, pairs)
        hit = facts_ref[pl.ds(HITS + k, 1), 0:1]
        rows_ref[pl.ds(start, pairs), :] = jnp.where(hit > 0, tile, 0.0)

    place(0, mine_ref[...])
    place(2 * len(fetched) + 1, last_ref[...])
    for i, (fetched_ref, handed_ref) in enumerate(zip(fetched, handed)):
        place(2 * i + 1 + my_core, fetched_ref[my_core])
        place(2 * i + 2 - my_core, handed_ref[...])
    amp_high, amp_low = high_and_low(rows_ref[...])
    amps = jnp.concatenate([amp_high, amp_low], axis=0)
    first = 0
    for high_ref, low_ref in ((high_a_ref, low_a_ref), (high_b_ref, low_b_ref)):
        for j in range(high_ref.shape[0] // LANES):
            part = slice(j * LANES, (j + 1) * LANES)
            term = lax.dot_general(
                high_ref[part, :], amps, CONTRACT_LAST, preferred_element_type=jnp.float32
            ) + lax.dot_general(
                low_ref[part, :], amps, CONTRACT_LAST, preferred_element_type=jnp.float32
            )
            term = term.T
            out_ref[:, first + j, :] = term[:total] + term[total:]
        first += high_ref.shape[0] // LANES


def on_device(amps, amp_tile, ints, tasks, pair_energy, virt_energy):
    nodes, devs = lax.axis_size("node"), lax.axis_size("dev")
    pairs, width = amps.shape[2], amps.shape[3]
    groups = width // LANES
    tile = jax.ShapeDtypeStruct((pairs, width), jnp.float32)
    task_rows = jnp.swapaxes(tasks, 1, 2)

    own = amps[0, 0]
    others = [
        lax.ppermute(own, "dev", [(i, i ^ k) for i in range(devs)]) for k in range(2, devs, 2)
    ]
    half = jax.ShapeDtypeStruct((width // 2, width), jnp.bfloat16)
    landing = [pltpu.VMEM(half.shape, jnp.float32), pltpu.SemaphoreType.DMA((CHUNKS,))]
    facts, denom, own, high_a, low_a = call(
        stage_kernel,
        "stage",
        (
            jax.ShapeDtypeStruct((HITS + nodes, LANES), jnp.int32),
            jax.ShapeDtypeStruct((nodes, groups, LANES), jnp.float32),
            tile,
            half,
            half,
        ),
        [pl.BlockSpec(memory_space=pltpu.SMEM)] + [HBM] * 5,
        [
            pltpu.VMEM(amp_tile.shape, jnp.int32),
            pltpu.VMEM(task_rows.shape, jnp.int32),
            pltpu.VMEM(virt_energy.shape, jnp.float32),
            pltpu.SemaphoreType.DMA((4,)),
            *landing,
        ],
        flops=width * width,
        moved=4 * width * width,
    )(pair_energy, *map(in_hbm, (amp_tile, task_rows, virt_energy, own, ints[0, 0])))
    slots = [own, *others]
    both = jax.ShapeDtypeStruct((2, pairs, width), jnp.float32)
    swap = [(i, i ^ 1) for i in range(devs)]
    held = call(pick_kernel, "pick", both, [VMEM] * (1 + len(slots)))(facts, *slots)
    got = lax.ppermute(held, "dev", swap)
    chip_tiles, mine = call(merge_kernel, "merge", (both, tile), [VMEM] * 3)(facts, held, got)

    fetched = [
        lax.ppermute(
            chip_tiles,
            ("node", "dev"),
            [
                (n * devs + d, (n ^ (k + d % 2)) * devs + d)
                for n in range(nodes)
                for d in range(devs)
            ],
        )
        for k in range(1, nodes - 1, 2)
    ]
    last = lax.ppermute(mine, "node", [(i, i ^ (nodes - 1)) for i in range(nodes)])
    high_b, low_b = call(
        split_kernel,
        "split",
        (half, half),
        [VMEM, HBM],
        landing,
        flops=width * width,
        moved=4 * width * width,
    )(mine, in_hbm(ints[0, 0]))
    handed = [
        lax.ppermute(call(theirs_kernel, "theirs", tile, [VMEM] * 2)(high_b, tiles), "dev", swap)
        for tiles in fetched
    ]
    products = call(
        product_kernel,
        "product",
        jax.ShapeDtypeStruct((nodes * pairs, groups, LANES), jnp.float32),
        [VMEM] * (7 + 2 * len(fetched)),
        [pltpu.VMEM((nodes * pairs, width), jnp.float32)],
        flops=6 * nodes * pairs * width * width,
        moved=4 * width * width,
    )(facts, high_a, low_a, high_b, low_b, mine, last, *fetched, *handed)

    terms = lax.all_to_all(products, ("node", "dev"), 0, 0, tiled=True)
    ladder = jnp.sum(terms.reshape(nodes, devs, groups, LANES), axis=1)
    return (ladder / denom).reshape(1, 1, nodes * width)


def solution(mesh):
    in_specs = (
        P("node", "dev", None, None),
        P(),
        P("node", "dev", None, None),
        P(),
        P("node", "dev"),
        P(),
    )
    return jax.shard_map(
        on_device, mesh=mesh, in_specs=in_specs, out_specs=P("node", "dev", None), check_vma=False
    )
```

```python
import jax
import jax.numpy as jnp
from jax import lax
from jax.experimental import pallas as pl
from jax.experimental.pallas import tpu as pltpu
from jax.sharding import PartitionSpec as P

LANES = 128
VMEM_LIMIT = 24 * 2**20
HITS = 2
VMEM = pl.BlockSpec(memory_space=pltpu.VMEM)
HBM = pl.BlockSpec(memory_space=pltpu.HBM)
CHUNKS = 2


def call(kernel, name, out_shape, in_specs, scratch=(), flops=0, moved=0):
    return pl.pallas_call(
        kernel,
        out_shape=out_shape,
        in_specs=in_specs,
        out_specs=jax.tree.map(lambda _: VMEM, out_shape),
        scratch_shapes=list(scratch),
        compiler_params=pltpu.CompilerParams(vmem_limit_bytes=VMEM_LIMIT),
        cost_estimate=pl.CostEstimate(flops=flops, bytes_accessed=moved, transcendentals=0),
        name=name,
    )


def high_and_low(x):
    high = x.astype(jnp.bfloat16)
    return high, (x - high.astype(jnp.float32)).astype(jnp.bfloat16)


def split_rows(ints_hbm, first, land_ref, sems, high_ref, low_ref):
    chunks = sems.shape[0]
    rows = high_ref.shape[1] // chunks
    copies = [
        pltpu.make_async_copy(
            ints_hbm.at[pl.ds(first + i * rows, rows)], land_ref.at[pl.ds(i * rows, rows)], sems.at[i]
        )
        for i in range(chunks)
    ]
    for copy in copies:
        copy.start()

    def finish():
        for i, copy in enumerate(copies):
            copy.wait()
            part = slice(i * rows, (i + 1) * rows)
            high_ref[:, part], low_ref[:, part] = high_and_low(land_ref[part, :].T)

    return finish


def in_hbm(x):
    return pltpu.with_memory_space_constraint(x, pltpu.HBM)


def stage_kernel(
    pair_ref, tile_hbm, tasks_hbm, virt_hbm, amps_hbm, ints_hbm,
    facts_ref, denom_ref, own_ref, high_ref, low_ref,
    tile_ref, tasks_ref, virt_ref, sems, land_ref, ints_sems,
):
    copies = [
        pltpu.make_async_copy(src, dst, sems.at[i])
        for i, (src, dst) in enumerate(
            [
                (tile_hbm, tile_ref),
                (tasks_hbm, tasks_ref),
                (virt_hbm, virt_ref),
                (amps_hbm, own_ref),
            ]
        )
    ]
    for copy in copies:
        copy.start()
    finish = split_rows(ints_hbm, 0, land_ref, ints_sems, high_ref, low_ref)
    my_node, my_dev = lax.axis_index("node"), lax.axis_index("dev")
    nodes = tasks_ref.shape[0]
    for copy in copies:
        copy.wait()
    row = tile_ref[pl.ds(my_node, 1), :]
    position = lax.broadcasted_iota(jnp.int32, row.shape, 1)
    for core in range(2):
        owner = my_dev // 2 * 2 + core
        slot = jnp.sum(jnp.where(row == owner, position, 0), axis=1, keepdims=True)
        facts_ref[core : core + 1, :] = jnp.broadcast_to(slot, (1, LANES))
    for k in range(nodes):
        task = tasks_ref[my_node ^ k]
        hit = jnp.where((task[0:1] == my_node) & (task[1:2] == my_dev), 1, 0)
        hit = jnp.max(hit, axis=1, keepdims=True)
        facts_ref[HITS + k : HITS + k + 1, :] = jnp.broadcast_to(hit, (1, LANES))
    denom = pair_ref[0, 0] - virt_ref[...]
    for j in range(denom_ref.shape[1]):
        denom_ref[:, j, :] = denom[:, j * LANES : (j + 1) * LANES]
    finish()


def split_kernel(after_ref, ints_hbm, high_ref, low_ref, land_ref, sems):
    del after_ref
    split_rows(ints_hbm, ints_hbm.shape[0] - high_ref.shape[1], land_ref, sems, high_ref, low_ref)()


def pick_kernel(facts_ref, *refs):
    pieces, held_ref = refs[:-1], refs[-1]
    chip = lax.axis_index("dev") // 2
    for core in range(2):
        step = (facts_ref[core : core + 1, 0:1] // 2) ^ chip
        tile = pieces[0][...]
        for j, piece in enumerate(pieces[1:], 1):
            tile = jnp.where(step == j, piece[...], tile)
        held_ref[core] = tile


def merge_kernel(facts_ref, held_ref, got_ref, both_ref, mine_ref):
    my_core = lax.axis_index("dev") % 2
    for core in range(2):
        here = facts_ref[core : core + 1, 0:1] % 2 == my_core
        both_ref[core] = jnp.where(here, held_ref[core], got_ref[core])
    mine_ref[...] = both_ref[my_core]


def theirs_kernel(after_ref, both_ref, theirs_ref):
    del after_ref
    theirs_ref[...] = both_ref[1 - lax.axis_index("dev") % 2]


def product_kernel(facts_ref, high_a_ref, low_a_ref, high_b_ref, low_b_ref, mine_ref, last_ref, *refs):
    fetched, handed = refs[: len(refs) // 2 - 1], refs[len(refs) // 2 - 1 : -2]
    out_ref, rows_ref = refs[-2:]
    my_node, my_core = lax.axis_index("node"), lax.axis_index("dev") % 2
    pairs = mine_ref.shape[0]
    total = rows_ref.shape[0]

    def place(k, tile):
        start = pl.multiple_of((my_node ^ k) * pairs, pairs)
        hit = facts_ref[pl.ds(HITS + k, 1), 0:1]
        rows_ref[pl.ds(start, pairs), :] = jnp.where(hit > 0, tile, 0.0)

    place(0, mine_ref[...])
    place(2 * len(fetched) + 1, last_ref[...])
    for i, (fetched_ref, handed_ref) in enumerate(zip(fetched, handed)):
        place(2 * i + 1 + my_core, fetched_ref[my_core])
        place(2 * i + 2 - my_core, handed_ref[...])
    amp_high, amp_low = high_and_low(rows_ref[...])
    amp_both = jnp.concatenate([amp_high, amp_low], axis=0)
    first = 0
    for high_ref, low_ref in ((high_a_ref, low_a_ref), (high_b_ref, low_b_ref)):
        both = jnp.dot(amp_both, high_ref[...], preferred_element_type=jnp.float32)
        rest = jnp.dot(amp_high, low_ref[...], preferred_element_type=jnp.float32)
        result = both[:total] + (both[total:] + rest)
        for j in range(high_ref.shape[1] // LANES):
            out_ref[:, first + j, :] = result[:, j * LANES : (j + 1) * LANES]
        first += high_ref.shape[1] // LANES


def on_device(amps, amp_tile, ints, tasks, pair_energy, virt_energy):
    nodes, devs = lax.axis_size("node"), lax.axis_size("dev")
    pairs, width = amps.shape[2], amps.shape[3]
    groups = width // LANES
    tile = jax.ShapeDtypeStruct((pairs, width), jnp.float32)
    task_rows = jnp.swapaxes(tasks, 1, 2)

    own = amps[0, 0]
    others = [
        lax.ppermute(own, "dev", [(i, i ^ k) for i in range(devs)]) for k in range(2, devs, 2)
    ]
    half = jax.ShapeDtypeStruct((width, width // 2), jnp.bfloat16)
    landing = [pltpu.VMEM((width // 2, width), jnp.float32), pltpu.SemaphoreType.DMA((CHUNKS,))]
    facts, denom, own, high_a, low_a = call(
        stage_kernel,
        "stage",
        (
            jax.ShapeDtypeStruct((HITS + nodes, LANES), jnp.int32),
            jax.ShapeDtypeStruct((nodes, groups, LANES), jnp.float32),
            tile,
            half,
            half,
        ),
        [pl.BlockSpec(memory_space=pltpu.SMEM)] + [HBM] * 5,
        [
            pltpu.VMEM(amp_tile.shape, jnp.int32),
            pltpu.VMEM(task_rows.shape, jnp.int32),
            pltpu.VMEM(virt_energy.shape, jnp.float32),
            pltpu.SemaphoreType.DMA((4,)),
            *landing,
        ],
        flops=width * width,
        moved=4 * width * width,
    )(pair_energy, *map(in_hbm, (amp_tile, task_rows, virt_energy, own, ints[0, 0])))
    slots = [own, *others]
    both = jax.ShapeDtypeStruct((2, pairs, width), jnp.float32)
    swap = [(i, i ^ 1) for i in range(devs)]
    held = call(pick_kernel, "pick", both, [VMEM] * (1 + len(slots)))(facts, *slots)
    got = lax.ppermute(held, "dev", swap)
    chip_tiles, mine = call(merge_kernel, "merge", (both, tile), [VMEM] * 3)(facts, held, got)

    fetched = [
        lax.ppermute(
            chip_tiles,
            ("node", "dev"),
            [
                (n * devs + d, (n ^ (k + d % 2)) * devs + d)
                for n in range(nodes)
                for d in range(devs)
            ],
        )
        for k in range(1, nodes - 1, 2)
    ]
    last = lax.ppermute(mine, "node", [(i, i ^ (nodes - 1)) for i in range(nodes)])
    high_b, low_b = call(
        split_kernel,
        "split",
        (half, half),
        [VMEM, HBM],
        landing,
        flops=width * width,
        moved=4 * width * width,
    )(mine, in_hbm(ints[0, 0]))
    handed = [
        lax.ppermute(call(theirs_kernel, "theirs", tile, [VMEM] * 2)(high_b, tiles), "dev", swap)
        for tiles in fetched
    ]
    products = call(
        product_kernel,
        "product",
        jax.ShapeDtypeStruct((nodes * pairs, groups, LANES), jnp.float32),
        [VMEM] * (7 + 2 * len(fetched)),
        [pltpu.VMEM((nodes * pairs, width), jnp.float32)],
        flops=6 * nodes * pairs * width * width,
        moved=4 * width * width,
    )(facts, high_a, low_a, high_b, low_b, mine, last, *fetched, *handed)

    terms = lax.all_to_all(products, ("node", "dev"), 0, 0, tiled=True)
    ladder = jnp.sum(terms.reshape(nodes, devs, groups, LANES), axis=1)
    return (ladder / denom).reshape(1, 1, nodes * width)


def solution(mesh):
    in_specs = (
        P("node", "dev", None, None),
        P(),
        P("node", "dev", None, None),
        P(),
        P("node", "dev"),
        P(),
    )
    return jax.shard_map(
        on_device, mesh=mesh, in_specs=in_specs, out_specs=P("node", "dev", None), check_vma=False
    )
```

```python
import jax
import jax.numpy as jnp
from jax import lax
from jax.experimental import pallas as pl
from jax.experimental.pallas import tpu as pltpu
from jax.sharding import PartitionSpec as P

LANES = 128
VMEM_LIMIT = 24 * 2**20
HITS = 2
VMEM = pl.BlockSpec(memory_space=pltpu.VMEM)
HBM = pl.BlockSpec(memory_space=pltpu.HBM)


def call(kernel, name, out_shape, in_specs, scratch=(), flops=0, moved=0):
    return pl.pallas_call(
        kernel,
        out_shape=out_shape,
        in_specs=in_specs,
        out_specs=jax.tree.map(lambda _: VMEM, out_shape),
        scratch_shapes=list(scratch),
        compiler_params=pltpu.CompilerParams(vmem_limit_bytes=VMEM_LIMIT),
        cost_estimate=pl.CostEstimate(flops=flops, bytes_accessed=moved, transcendentals=0),
        name=name,
    )


def high_and_low(x):
    high = x.astype(jnp.bfloat16)
    return high, (x - high.astype(jnp.float32)).astype(jnp.bfloat16)


def split_rows(ints_hbm, first, land_ref, sems, high_ref, low_ref):
    chunks = sems.shape[0]
    rows = high_ref.shape[1] // chunks
    copies = [
        pltpu.make_async_copy(
            ints_hbm.at[pl.ds(first + i * rows, rows)], land_ref.at[pl.ds(i * rows, rows)], sems.at[i]
        )
        for i in range(chunks)
    ]
    for copy in copies:
        copy.start()

    def finish():
        for i, copy in enumerate(copies):
            copy.wait()
            part = slice(i * rows, (i + 1) * rows)
            high_ref[:, part], low_ref[:, part] = high_and_low(land_ref[part, :].T)

    return finish


def in_hbm(x):
    return pltpu.with_memory_space_constraint(x, pltpu.HBM)


def stage_kernel(
    pair_ref, tile_hbm, tasks_hbm, virt_hbm, amps_hbm, ints_hbm,
    facts_ref, denom_ref, own_ref, high_ref, low_ref,
    tile_ref, tasks_ref, virt_ref, sems, land_ref, ints_sems,
):
    copies = [
        pltpu.make_async_copy(src, dst, sems.at[i])
        for i, (src, dst) in enumerate(
            [
                (tile_hbm, tile_ref),
                (tasks_hbm, tasks_ref),
                (virt_hbm, virt_ref),
                (amps_hbm, own_ref),
            ]
        )
    ]
    for copy in copies:
        copy.start()
    finish = split_rows(ints_hbm, 0, land_ref, ints_sems, high_ref, low_ref)
    my_node, my_dev = lax.axis_index("node"), lax.axis_index("dev")
    nodes = tasks_ref.shape[0]
    for copy in copies:
        copy.wait()
    row = tile_ref[pl.ds(my_node, 1), :]
    position = lax.broadcasted_iota(jnp.int32, row.shape, 1)
    for core in range(2):
        owner = my_dev // 2 * 2 + core
        slot = jnp.sum(jnp.where(row == owner, position, 0), axis=1, keepdims=True)
        facts_ref[core : core + 1, :] = jnp.broadcast_to(slot, (1, LANES))
    for k in range(nodes):
        task = tasks_ref[my_node ^ k]
        hit = jnp.where((task[0:1] == my_node) & (task[1:2] == my_dev), 1, 0)
        hit = jnp.max(hit, axis=1, keepdims=True)
        facts_ref[HITS + k : HITS + k + 1, :] = jnp.broadcast_to(hit, (1, LANES))
    denom = pair_ref[0, 0] - virt_ref[...]
    for j in range(denom_ref.shape[1]):
        denom_ref[:, j, :] = denom[:, j * LANES : (j + 1) * LANES]
    finish()


def split_kernel(after_ref, ints_hbm, high_ref, low_ref, land_ref, sems):
    del after_ref
    split_rows(ints_hbm, ints_hbm.shape[0] - high_ref.shape[1], land_ref, sems, high_ref, low_ref)()


def pick_kernel(facts_ref, *refs):
    pieces, held_ref = refs[:-1], refs[-1]
    chip = lax.axis_index("dev") // 2
    for core in range(2):
        step = (facts_ref[core : core + 1, 0:1] // 2) ^ chip
        tile = pieces[0][...]
        for j, piece in enumerate(pieces[1:], 1):
            tile = jnp.where(step == j, piece[...], tile)
        held_ref[core] = tile


def merge_kernel(facts_ref, held_ref, got_ref, both_ref, mine_ref, theirs_ref):
    my_dev = lax.axis_index("dev")
    my_core = my_dev % 2
    for core in range(2):
        slot = facts_ref[core : core + 1, 0:1]
        here = (slot % 2 == my_core) == (slot // 2 == my_dev // 2)
        both_ref[core] = jnp.where(here, held_ref[core], got_ref[core])
    mine_ref[...] = both_ref[my_core]
    theirs_ref[...] = both_ref[1 - my_core]


def theirs_kernel(after_ref, both_ref, theirs_ref):
    del after_ref
    theirs_ref[...] = both_ref[1 - lax.axis_index("dev") % 2]


def product_kernel(facts_ref, high_a_ref, low_a_ref, high_b_ref, low_b_ref, mine_ref, last_ref, *refs):
    fetched, handed = refs[: len(refs) // 2 - 1], refs[len(refs) // 2 - 1 : -2]
    out_ref, rows_ref = refs[-2:]
    my_node, my_core = lax.axis_index("node"), lax.axis_index("dev") % 2
    pairs = mine_ref.shape[0]
    total = rows_ref.shape[0]

    def place(k, tile):
        start = pl.multiple_of((my_node ^ k) * pairs, pairs)
        hit = facts_ref[pl.ds(HITS + k, 1), 0:1]
        rows_ref[pl.ds(start, pairs), :] = jnp.where(hit > 0, tile, 0.0)

    place(0, mine_ref[...])
    place(2 * len(fetched) + 1, last_ref[...])
    for i, (fetched_ref, handed_ref) in enumerate(zip(fetched, handed)):
        place(2 * i + 1 + my_core, fetched_ref[my_core])
        place(2 * i + 2 - my_core, handed_ref[...])
    amp_high, amp_low = high_and_low(rows_ref[...])
    amp_both = jnp.concatenate([amp_high, amp_low], axis=0)
    first = 0
    for high_ref, low_ref in ((high_a_ref, low_a_ref), (high_b_ref, low_b_ref)):
        both = jnp.dot(amp_both, high_ref[...], preferred_element_type=jnp.float32)
        rest = jnp.dot(amp_high, low_ref[...], preferred_element_type=jnp.float32)
        result = both[:total] + (both[total:] + rest)
        for j in range(high_ref.shape[1] // LANES):
            out_ref[:, first + j, :] = result[:, j * LANES : (j + 1) * LANES]
        first += high_ref.shape[1] // LANES


def on_device(amps, amp_tile, ints, tasks, pair_energy, virt_energy):
    nodes, devs = lax.axis_size("node"), lax.axis_size("dev")
    pairs, width = amps.shape[2], amps.shape[3]
    groups = width // LANES
    tile = jax.ShapeDtypeStruct((pairs, width), jnp.float32)
    task_rows = jnp.swapaxes(tasks, 1, 2)

    own = amps[0, 0]
    others = [
        lax.ppermute(own, "dev", [(i, i ^ k) for i in range(devs)]) for k in range(3, devs, 2)
    ]
    chunk = width // 4

    def part(chunks):
        return jax.ShapeDtypeStruct((width, chunks * chunk), jnp.bfloat16), [
            pltpu.VMEM((chunks * chunk, width), jnp.float32),
            pltpu.SemaphoreType.DMA((chunks,)),
        ]

    early, early_landing = part(1)
    late, late_landing = part(3)
    facts, denom, own, high_a, low_a = call(
        stage_kernel,
        "stage",
        (
            jax.ShapeDtypeStruct((HITS + nodes, LANES), jnp.int32),
            jax.ShapeDtypeStruct((nodes, groups, LANES), jnp.float32),
            tile,
            early,
            early,
        ),
        [pl.BlockSpec(memory_space=pltpu.SMEM)] + [HBM] * 5,
        [
            pltpu.VMEM(amp_tile.shape, jnp.int32),
            pltpu.VMEM(task_rows.shape, jnp.int32),
            pltpu.VMEM(virt_energy.shape, jnp.float32),
            pltpu.SemaphoreType.DMA((4,)),
            *early_landing,
        ],
        flops=width * width,
        moved=4 * width * width,
    )(pair_energy, *map(in_hbm, (amp_tile, task_rows, virt_energy, own, ints[0, 0])))
    slots = [own, *others]
    both = jax.ShapeDtypeStruct((2, pairs, width), jnp.float32)
    swap = [(i, i ^ 1) for i in range(devs)]
    held = call(pick_kernel, "pick", both, [VMEM] * (1 + len(slots)))(facts, *slots)
    got = lax.ppermute(held, "dev", swap)
    chip_tiles, mine, theirs = call(merge_kernel, "merge", (both, tile, tile), [VMEM] * 3)(facts, held, got)

    fetched = [
        lax.ppermute(
            chip_tiles,
            ("node", "dev"),
            [
                (n * devs + d, (n ^ (k + d % 2)) * devs + d)
                for n in range(nodes)
                for d in range(devs)
            ],
        )
        for k in range(1, nodes - 1, 2)
    ]
    last = lax.ppermute(
        theirs,
        ("node", "dev"),
        [
            (n * devs + d, (n ^ (nodes - 1)) * devs + (d ^ 1))
            for n in range(nodes)
            for d in range(devs)
        ],
    )
    high_b, low_b = call(
        split_kernel,
        "split",
        (late, late),
        [VMEM, HBM],
        late_landing,
        flops=width * width,
        moved=4 * width * width,
    )(mine, in_hbm(ints[0, 0]))
    handed = [
        lax.ppermute(call(theirs_kernel, "theirs", tile, [VMEM] * 2)(high_b, tiles), "dev", swap)
        for tiles in fetched
    ]
    products = call(
        product_kernel,
        "product",
        jax.ShapeDtypeStruct((nodes * pairs, groups, LANES), jnp.float32),
        [VMEM] * (7 + 2 * len(fetched)),
        [pltpu.VMEM((nodes * pairs, width), jnp.float32)],
        flops=6 * nodes * pairs * width * width,
        moved=4 * width * width,
    )(facts, high_a, low_a, high_b, low_b, mine, last, *fetched, *handed)

    terms = lax.all_to_all(products, ("node", "dev"), 0, 0, tiled=True)
    ladder = jnp.sum(terms.reshape(nodes, devs, groups, LANES), axis=1)
    return (ladder / denom).reshape(1, 1, nodes * width)


def solution(mesh):
    in_specs = (
        P("node", "dev", None, None),
        P(),
        P("node", "dev", None, None),
        P(),
        P("node", "dev"),
        P(),
    )
    return jax.shard_map(
        on_device, mesh=mesh, in_specs=in_specs, out_specs=P("node", "dev", None), check_vma=False
    )
```

```python
import functools
import math

import jax
import jax.numpy as jnp
from jax import lax
from jax.experimental import pallas as pl
from jax.experimental.pallas import tpu as pltpu
from jax.sharding import PartitionSpec as P

LANES = 128
VMEM_LIMIT = 24 * 2**20
HITS = 2
VMEM = pl.BlockSpec(memory_space=pltpu.VMEM)
HBM = pl.BlockSpec(memory_space=pltpu.HBM)


def exchange_order(total):
    step = total - 5 if math.gcd(5, total) == 1 else 1
    return [(j * step) % total for j in range(total)]


def call(kernel, name, out_shape, in_specs, scratch=(), flops=0, moved=0):
    return pl.pallas_call(
        kernel,
        out_shape=out_shape,
        in_specs=in_specs,
        out_specs=jax.tree.map(lambda _: VMEM, out_shape),
        scratch_shapes=list(scratch),
        compiler_params=pltpu.CompilerParams(vmem_limit_bytes=VMEM_LIMIT),
        cost_estimate=pl.CostEstimate(flops=flops, bytes_accessed=moved, transcendentals=0),
        name=name,
    )


def high_and_low(x):
    high = x.astype(jnp.bfloat16)
    return high, (x - high.astype(jnp.float32)).astype(jnp.bfloat16)


def split_rows(ints_hbm, first, land_ref, sems, high_ref, low_ref):
    chunks = sems.shape[0]
    rows = high_ref.shape[1] // chunks
    copies = [
        pltpu.make_async_copy(
            ints_hbm.at[pl.ds(first + i * rows, rows)], land_ref.at[pl.ds(i * rows, rows)], sems.at[i]
        )
        for i in range(chunks)
    ]
    for copy in copies:
        copy.start()

    def finish():
        for i, copy in enumerate(copies):
            copy.wait()
            part = slice(i * rows, (i + 1) * rows)
            high_ref[:, part], low_ref[:, part] = high_and_low(land_ref[part, :].T)

    return finish


def in_hbm(x):
    return pltpu.with_memory_space_constraint(x, pltpu.HBM)


def stage_kernel(
    pair_ref, tile_hbm, tasks_hbm, virt_hbm, amps_hbm, ints_hbm,
    facts_ref, denom_ref, own_ref, high_ref, low_ref,
    tile_ref, tasks_ref, virt_ref, sems, land_ref, ints_sems,
):
    copies = [
        pltpu.make_async_copy(src, dst, sems.at[i])
        for i, (src, dst) in enumerate(
            [
                (tile_hbm, tile_ref),
                (tasks_hbm, tasks_ref),
                (virt_hbm, virt_ref),
                (amps_hbm, own_ref),
            ]
        )
    ]
    for copy in copies:
        copy.start()
    finish = split_rows(ints_hbm, 0, land_ref, ints_sems, high_ref, low_ref)
    my_node, my_dev = lax.axis_index("node"), lax.axis_index("dev")
    nodes = tasks_ref.shape[0]
    for copy in copies:
        copy.wait()
    row = tile_ref[pl.ds(my_node, 1), :]
    position = lax.broadcasted_iota(jnp.int32, row.shape, 1)
    for core in range(2):
        owner = my_dev // 2 * 2 + core
        slot = jnp.sum(jnp.where(row == owner, position, 0), axis=1, keepdims=True)
        facts_ref[core : core + 1, :] = jnp.broadcast_to(slot, (1, LANES))
    for k in range(nodes):
        task = tasks_ref[my_node ^ k]
        hit = jnp.where((task[0:1] == my_node) & (task[1:2] == my_dev), 1, 0)
        hit = jnp.max(hit, axis=1, keepdims=True)
        facts_ref[HITS + k : HITS + k + 1, :] = jnp.broadcast_to(hit, (1, LANES))
    denom = pair_ref[0, 0] - virt_ref[...]
    for j in range(denom_ref.shape[1]):
        denom_ref[:, j, :] = denom[:, j * LANES : (j + 1) * LANES]
    finish()


def split_kernel(after_ref, ints_hbm, high_ref, low_ref, land_ref, sems):
    del after_ref
    split_rows(ints_hbm, ints_hbm.shape[0] - high_ref.shape[1], land_ref, sems, high_ref, low_ref)()


def pick_kernel(facts_ref, *refs):
    pieces, held_ref = refs[:-1], refs[-1]
    chip = lax.axis_index("dev") // 2
    for core in range(2):
        step = (facts_ref[core : core + 1, 0:1] // 2) ^ chip
        tile = pieces[0][...]
        for j, piece in enumerate(pieces[1:], 1):
            tile = jnp.where(step == j, piece[...], tile)
        held_ref[core] = tile


def merge_kernel(facts_ref, held_ref, got_ref, both_ref, mine_ref, theirs_ref):
    my_dev = lax.axis_index("dev")
    my_core = my_dev % 2
    for core in range(2):
        slot = facts_ref[core : core + 1, 0:1]
        here = (slot % 2 == my_core) == (slot // 2 == my_dev // 2)
        both_ref[core] = jnp.where(here, held_ref[core], got_ref[core])
    mine_ref[...] = both_ref[my_core]
    theirs_ref[...] = both_ref[1 - my_core]


def theirs_kernel(after_ref, both_ref, theirs_ref):
    del after_ref
    theirs_ref[...] = both_ref[1 - lax.axis_index("dev") % 2]


def product_kernel(facts_ref, high_a_ref, low_a_ref, high_b_ref, low_b_ref, mine_ref, last_ref, *refs):
    fetched, handed = refs[: len(refs) // 2 - 1], refs[len(refs) // 2 - 1 : -2]
    out_ref, rows_ref = refs[-2:]
    my_node, my_core = lax.axis_index("node"), lax.axis_index("dev") % 2
    pairs = mine_ref.shape[0]
    total = rows_ref.shape[0]

    def place(k, tile):
        start = pl.multiple_of((my_node ^ k) * pairs, pairs)
        hit = facts_ref[pl.ds(HITS + k, 1), 0:1]
        rows_ref[pl.ds(start, pairs), :] = jnp.where(hit > 0, tile, 0.0)

    place(0, mine_ref[...])
    place(2 * len(fetched) + 1, last_ref[...])
    for i, (fetched_ref, handed_ref) in enumerate(zip(fetched, handed)):
        place(2 * i + 1 + my_core, fetched_ref[my_core])
        place(2 * i + 2 - my_core, handed_ref[...])
    amp_high, amp_low = high_and_low(rows_ref[...])
    amp_both = jnp.concatenate([amp_high, amp_low], axis=0)
    first = 0
    for high_ref, low_ref in ((high_a_ref, low_a_ref), (high_b_ref, low_b_ref)):
        both = jnp.dot(amp_both, high_ref[...], preferred_element_type=jnp.float32)
        rest = jnp.dot(amp_high, low_ref[...], preferred_element_type=jnp.float32)
        result = both[:total] + (both[total:] + rest)
        for position, row in enumerate(exchange_order(total)):
            for j in range(high_ref.shape[1] // LANES):
                out_ref[position, first + j, :] = result[row, j * LANES : (j + 1) * LANES]
        first += high_ref.shape[1] // LANES


def resid_kernel(devs, terms_ref, denom_ref, resid_ref):
    sums = [None] * resid_ref.shape[0]
    for position, device in enumerate(exchange_order(terms_ref.shape[0])):
        node, term = device // devs, terms_ref[position]
        sums[node] = term if sums[node] is None else sums[node] + term
    for node, total in enumerate(sums):
        resid_ref[node] = total / denom_ref[node]


def on_device(amps, amp_tile, ints, tasks, pair_energy, virt_energy):
    nodes, devs = lax.axis_size("node"), lax.axis_size("dev")
    pairs, width = amps.shape[2], amps.shape[3]
    groups = width // LANES
    tile = jax.ShapeDtypeStruct((pairs, width), jnp.float32)
    task_rows = jnp.swapaxes(tasks, 1, 2)

    own = amps[0, 0]
    others = [
        lax.ppermute(own, "dev", [(i, i ^ k) for i in range(devs)]) for k in range(3, devs, 2)
    ]
    chunk = width // 4

    def part(chunks):
        return jax.ShapeDtypeStruct((width, chunks * chunk), jnp.bfloat16), [
            pltpu.VMEM((chunks * chunk, width), jnp.float32),
            pltpu.SemaphoreType.DMA((chunks,)),
        ]

    early, early_landing = part(1)
    late, late_landing = part(3)
    facts, denom, own, high_a, low_a = call(
        stage_kernel,
        "stage",
        (
            jax.ShapeDtypeStruct((HITS + nodes, LANES), jnp.int32),
            jax.ShapeDtypeStruct((nodes, groups, LANES), jnp.float32),
            tile,
            early,
            early,
        ),
        [pl.BlockSpec(memory_space=pltpu.SMEM)] + [HBM] * 5,
        [
            pltpu.VMEM(amp_tile.shape, jnp.int32),
            pltpu.VMEM(task_rows.shape, jnp.int32),
            pltpu.VMEM(virt_energy.shape, jnp.float32),
            pltpu.SemaphoreType.DMA((4,)),
            *early_landing,
        ],
        flops=width * width,
        moved=4 * width * width,
    )(pair_energy, *map(in_hbm, (amp_tile, task_rows, virt_energy, own, ints[0, 0])))
    slots = [own, *others]
    both = jax.ShapeDtypeStruct((2, pairs, width), jnp.float32)
    swap = [(i, i ^ 1) for i in range(devs)]
    held = call(pick_kernel, "pick", both, [VMEM] * (1 + len(slots)))(facts, *slots)
    got = lax.ppermute(held, "dev", swap)
    chip_tiles, mine, theirs = call(merge_kernel, "merge", (both, tile, tile), [VMEM] * 3)(facts, held, got)

    fetched = [
        lax.ppermute(
            chip_tiles,
            ("node", "dev"),
            [
                (n * devs + d, (n ^ (k + d % 2)) * devs + d)
                for n in range(nodes)
                for d in range(devs)
            ],
        )
        for k in range(1, nodes - 1, 2)
    ]
    last = lax.ppermute(
        theirs,
        ("node", "dev"),
        [
            (n * devs + d, (n ^ (nodes - 1)) * devs + (d ^ 1))
            for n in range(nodes)
            for d in range(devs)
        ],
    )
    high_b, low_b = call(
        split_kernel,
        "split",
        (late, late),
        [VMEM, HBM],
        late_landing,
        flops=width * width,
        moved=4 * width * width,
    )(mine, in_hbm(ints[0, 0]))
    handed = [
        lax.ppermute(call(theirs_kernel, "theirs", tile, [VMEM] * 2)(high_b, tiles), "dev", swap)
        for tiles in fetched
    ]
    products = call(
        product_kernel,
        "product",
        jax.ShapeDtypeStruct((nodes * pairs, groups, LANES), jnp.float32),
        [VMEM] * (7 + 2 * len(fetched)),
        [pltpu.VMEM((nodes * pairs, width), jnp.float32)],
        flops=6 * nodes * pairs * width * width,
        moved=4 * width * width,
    )(facts, high_a, low_a, high_b, low_b, mine, last, *fetched, *handed)

    terms = lax.all_to_all(
        products,
        ("node", "dev"),
        0,
        0,
        tiled=True,
        axis_index_groups=[exchange_order(nodes * devs)],
    )
    resid = call(
        functools.partial(resid_kernel, devs),
        "resid",
        jax.ShapeDtypeStruct((nodes, groups, LANES), jnp.float32),
        [VMEM] * 2,
    )(terms, denom)
    return resid.reshape(1, 1, nodes * width)


def solution(mesh):
    in_specs = (
        P("node", "dev", None, None),
        P(),
        P("node", "dev", None, None),
        P(),
        P("node", "dev"),
        P(),
    )
    return jax.shard_map(
        on_device, mesh=mesh, in_specs=in_specs, out_specs=P("node", "dev", None), check_vma=False
    )
```

```python
import functools
import math

import jax
import jax.numpy as jnp
from jax import lax
from jax.experimental import pallas as pl
from jax.experimental.pallas import tpu as pltpu
from jax.sharding import PartitionSpec as P

LANES = 128
VMEM_LIMIT = 24 * 2**20
HITS = 2
VMEM = pl.BlockSpec(memory_space=pltpu.VMEM)
HBM = pl.BlockSpec(memory_space=pltpu.HBM)


def exchange_order(total):
    step = total - 5 if math.gcd(5, total) == 1 else 1
    return [(j * step) % total for j in range(total)]


def gather_steps(devs):
    odd = list(range(1, devs // 2))
    even = odd[1::-1] + odd[2:]
    return list(zip(even, odd))


def call(kernel, name, out_shape, in_specs, scratch=(), flops=0, moved=0):
    return pl.pallas_call(
        kernel,
        out_shape=out_shape,
        in_specs=in_specs,
        out_specs=jax.tree.map(lambda _: VMEM, out_shape),
        scratch_shapes=list(scratch),
        compiler_params=pltpu.CompilerParams(vmem_limit_bytes=VMEM_LIMIT),
        cost_estimate=pl.CostEstimate(flops=flops, bytes_accessed=moved, transcendentals=0),
        name=name,
    )


def high_and_low(x):
    high = x.astype(jnp.bfloat16)
    return high, (x - high.astype(jnp.float32)).astype(jnp.bfloat16)


def split_rows(ints_hbm, first, land_ref, sems, high_ref, low_ref):
    chunks = sems.shape[0]
    rows = high_ref.shape[1] // chunks
    copies = [
        pltpu.make_async_copy(
            ints_hbm.at[pl.ds(first + i * rows, rows)], land_ref.at[pl.ds(i * rows, rows)], sems.at[i]
        )
        for i in range(chunks)
    ]
    for copy in copies:
        copy.start()

    def finish():
        for i, copy in enumerate(copies):
            copy.wait()
            part = slice(i * rows, (i + 1) * rows)
            high_ref[:, part], low_ref[:, part] = high_and_low(land_ref[part, :].T)

    return finish


def in_hbm(x):
    return pltpu.with_memory_space_constraint(x, pltpu.HBM)


def stage_kernel(
    pair_ref, tile_hbm, tasks_hbm, virt_hbm, amps_hbm, ints_hbm,
    facts_ref, denom_ref, own_ref, high_ref, low_ref,
    tile_ref, tasks_ref, virt_ref, sems, land_ref, ints_sems,
):
    copies = [
        pltpu.make_async_copy(src, dst, sems.at[i])
        for i, (src, dst) in enumerate(
            [
                (tile_hbm, tile_ref),
                (tasks_hbm, tasks_ref),
                (virt_hbm, virt_ref),
                (amps_hbm, own_ref),
            ]
        )
    ]
    for copy in copies:
        copy.start()
    finish = split_rows(ints_hbm, 0, land_ref, ints_sems, high_ref, low_ref)
    my_node, my_dev = lax.axis_index("node"), lax.axis_index("dev")
    nodes = tasks_ref.shape[0]
    for copy in copies:
        copy.wait()
    row = tile_ref[pl.ds(my_node, 1), :]
    position = lax.broadcasted_iota(jnp.int32, row.shape, 1)
    for core in range(2):
        owner = my_dev // 2 * 2 + core
        slot = jnp.sum(jnp.where(row == owner, position, 0), axis=1, keepdims=True)
        facts_ref[core : core + 1, :] = jnp.broadcast_to(slot, (1, LANES))
    for k in range(nodes):
        task = tasks_ref[my_node ^ k]
        hit = jnp.where((task[0:1] == my_node) & (task[1:2] == my_dev), 1, 0)
        hit = jnp.max(hit, axis=1, keepdims=True)
        facts_ref[HITS + k : HITS + k + 1, :] = jnp.broadcast_to(hit, (1, LANES))
    denom = pair_ref[0, 0] - virt_ref[...]
    for j in range(denom_ref.shape[1]):
        denom_ref[:, j, :] = denom[:, j * LANES : (j + 1) * LANES]
    finish()


def split_kernel(after_ref, ints_hbm, high_ref, low_ref, land_ref, sems):
    del after_ref
    split_rows(ints_hbm, ints_hbm.shape[0] - high_ref.shape[1], land_ref, sems, high_ref, low_ref)()


def pick_kernel(facts_ref, own_ref, *refs):
    pieces, held_ref = refs[:-1], refs[-1]
    my_dev = lax.axis_index("dev")
    steps = [
        jnp.where(my_dev % 2 == 0, odd, even) for even, odd in gather_steps(2 * len(pieces) + 2)
    ]
    for core in range(2):
        wanted = (facts_ref[core : core + 1, 0:1] // 2) ^ (my_dev // 2)
        tile = own_ref[...]
        for step, piece in zip(steps, pieces):
            tile = jnp.where(wanted == step, piece[...], tile)
        held_ref[core] = tile


def merge_kernel(facts_ref, held_ref, got_ref, both_ref, mine_ref, theirs_ref):
    my_dev = lax.axis_index("dev")
    my_core = my_dev % 2
    for core in range(2):
        slot = facts_ref[core : core + 1, 0:1]
        here = (slot % 2 == my_core) == (slot // 2 == my_dev // 2)
        both_ref[core] = jnp.where(here, held_ref[core], got_ref[core])
    mine_ref[...] = both_ref[my_core]
    theirs_ref[...] = both_ref[1 - my_core]


def theirs_kernel(after_ref, both_ref, theirs_ref):
    del after_ref
    theirs_ref[...] = both_ref[1 - lax.axis_index("dev") % 2]


def product_kernel(facts_ref, high_a_ref, low_a_ref, high_b_ref, low_b_ref, mine_ref, last_ref, *refs):
    fetched, handed = refs[: len(refs) // 2 - 1], refs[len(refs) // 2 - 1 : -2]
    out_ref, rows_ref = refs[-2:]
    my_node, my_core = lax.axis_index("node"), lax.axis_index("dev") % 2
    pairs = mine_ref.shape[0]
    total = rows_ref.shape[0]

    def place(k, tile):
        start = pl.multiple_of((my_node ^ k) * pairs, pairs)
        hit = facts_ref[pl.ds(HITS + k, 1), 0:1]
        rows_ref[pl.ds(start, pairs), :] = jnp.where(hit > 0, tile, 0.0)

    place(0, mine_ref[...])
    place(2 * len(fetched) + 1, last_ref[...])
    for i, (fetched_ref, handed_ref) in enumerate(zip(fetched, handed)):
        place(2 * i + 1 + my_core, fetched_ref[my_core])
        place(2 * i + 2 - my_core, handed_ref[...])
    amp_high, amp_low = high_and_low(rows_ref[...])
    amp_both = jnp.concatenate([amp_high, amp_low], axis=0)
    first = 0
    for high_ref, low_ref in ((high_a_ref, low_a_ref), (high_b_ref, low_b_ref)):
        both = jnp.dot(amp_both, high_ref[...], preferred_element_type=jnp.float32)
        rest = jnp.dot(amp_high, low_ref[...], preferred_element_type=jnp.float32)
        result = both[:total] + (both[total:] + rest)
        for position, row in enumerate(exchange_order(total)):
            for j in range(high_ref.shape[1] // LANES):
                out_ref[position, first + j, :] = result[row, j * LANES : (j + 1) * LANES]
        first += high_ref.shape[1] // LANES


def resid_kernel(devs, terms_ref, denom_ref, resid_ref):
    sums = [None] * resid_ref.shape[0]
    for position, device in enumerate(exchange_order(terms_ref.shape[0])):
        node, term = device // devs, terms_ref[position]
        sums[node] = term if sums[node] is None else sums[node] + term
    for node, total in enumerate(sums):
        resid_ref[node] = total / denom_ref[node]


def on_device(amps, amp_tile, ints, tasks, pair_energy, virt_energy):
    nodes, devs = lax.axis_size("node"), lax.axis_size("dev")
    pairs, width = amps.shape[2], amps.shape[3]
    groups = width // LANES
    tile = jax.ShapeDtypeStruct((pairs, width), jnp.float32)
    task_rows = jnp.swapaxes(tasks, 1, 2)

    own = amps[0, 0]
    others = [
        lax.ppermute(own, "dev", [(i, i ^ (2 * steps[i % 2] + 1)) for i in range(devs)])
        for steps in gather_steps(devs)
    ]
    chunk = width // 4

    def part(chunks):
        return jax.ShapeDtypeStruct((width, chunks * chunk), jnp.bfloat16), [
            pltpu.VMEM((chunks * chunk, width), jnp.float32),
            pltpu.SemaphoreType.DMA((chunks,)),
        ]

    early, early_landing = part(1)
    late, late_landing = part(3)
    facts, denom, own, high_a, low_a = call(
        stage_kernel,
        "stage",
        (
            jax.ShapeDtypeStruct((HITS + nodes, LANES), jnp.int32),
            jax.ShapeDtypeStruct((nodes, groups, LANES), jnp.float32),
            tile,
            early,
            early,
        ),
        [pl.BlockSpec(memory_space=pltpu.SMEM)] + [HBM] * 5,
        [
            pltpu.VMEM(amp_tile.shape, jnp.int32),
            pltpu.VMEM(task_rows.shape, jnp.int32),
            pltpu.VMEM(virt_energy.shape, jnp.float32),
            pltpu.SemaphoreType.DMA((4,)),
            *early_landing,
        ],
        flops=width * width,
        moved=4 * width * width,
    )(pair_energy, *map(in_hbm, (amp_tile, task_rows, virt_energy, own, ints[0, 0])))
    both = jax.ShapeDtypeStruct((2, pairs, width), jnp.float32)
    swap = [(i, i ^ 1) for i in range(devs)]
    held = call(pick_kernel, "pick", both, [VMEM] * (2 + len(others)))(facts, own, *others)
    got = lax.ppermute(held, "dev", swap)
    chip_tiles, mine, theirs = call(merge_kernel, "merge", (both, tile, tile), [VMEM] * 3)(facts, held, got)

    fetched = [
        lax.ppermute(
            chip_tiles,
            ("node", "dev"),
            [
                (n * devs + d, (n ^ (k + d % 2)) * devs + d)
                for n in range(nodes)
                for d in range(devs)
            ],
        )
        for k in range(1, nodes - 1, 2)
    ]
    last = lax.ppermute(
        theirs,
        ("node", "dev"),
        [
            (n * devs + d, (n ^ (nodes - 1)) * devs + (d ^ 1))
            for n in range(nodes)
            for d in range(devs)
        ],
    )
    high_b, low_b = call(
        split_kernel,
        "split",
        (late, late),
        [VMEM, HBM],
        late_landing,
        flops=width * width,
        moved=4 * width * width,
    )(mine, in_hbm(ints[0, 0]))
    handed = [
        lax.ppermute(call(theirs_kernel, "theirs", tile, [VMEM] * 2)(high_b, tiles), "dev", swap)
        for tiles in fetched
    ]
    products = call(
        product_kernel,
        "product",
        jax.ShapeDtypeStruct((nodes * pairs, groups, LANES), jnp.float32),
        [VMEM] * (7 + 2 * len(fetched)),
        [pltpu.VMEM((nodes * pairs, width), jnp.float32)],
        flops=6 * nodes * pairs * width * width,
        moved=4 * width * width,
    )(facts, high_a, low_a, high_b, low_b, mine, last, *fetched, *handed)

    terms = lax.all_to_all(
        products,
        ("node", "dev"),
        0,
        0,
        tiled=True,
        axis_index_groups=[exchange_order(nodes * devs)],
    )
    resid = call(
        functools.partial(resid_kernel, devs),
        "resid",
        jax.ShapeDtypeStruct((nodes, groups, LANES), jnp.float32),
        [VMEM] * 2,
    )(terms, denom)
    return resid.reshape(1, 1, nodes * width)


def solution(mesh):
    in_specs = (
        P("node", "dev", None, None),
        P(),
        P("node", "dev", None, None),
        P(),
        P("node", "dev"),
        P(),
    )
    return jax.shard_map(
        on_device, mesh=mesh, in_specs=in_specs, out_specs=P("node", "dev", None), check_vma=False
    )
```

```python
import functools
import math

import jax
import jax.numpy as jnp
from jax import lax
from jax.experimental import pallas as pl
from jax.experimental.pallas import tpu as pltpu
from jax.sharding import PartitionSpec as P

LANES = 128
VMEM_LIMIT = 24 * 2**20
HITS = 2
VMEM = pl.BlockSpec(memory_space=pltpu.VMEM)
HBM = pl.BlockSpec(memory_space=pltpu.HBM)


def exchange_order(total):
    step = total - 5 if math.gcd(5, total) == 1 else 1
    return [(j * step) % total for j in range(total)]


def gather_steps(devs):
    odd = list(range(1, devs // 2))
    even = odd[1::-1] + odd[2:]
    return list(zip(even, odd))


def call(kernel, name, out_shape, in_specs, scratch=(), flops=0, moved=0):
    return pl.pallas_call(
        kernel,
        out_shape=out_shape,
        in_specs=in_specs,
        out_specs=jax.tree.map(lambda _: VMEM, out_shape),
        scratch_shapes=list(scratch),
        compiler_params=pltpu.CompilerParams(vmem_limit_bytes=VMEM_LIMIT),
        cost_estimate=pl.CostEstimate(flops=flops, bytes_accessed=moved, transcendentals=0),
        name=name,
    )


def high_and_low(x):
    high = x.astype(jnp.bfloat16)
    return high, (x - high.astype(jnp.float32)).astype(jnp.bfloat16)


def split_rows(ints_hbm, first, land_ref, sems, high_ref, low_ref):
    chunks = sems.shape[0]
    rows = high_ref.shape[1] // chunks
    copies = [
        pltpu.make_async_copy(
            ints_hbm.at[pl.ds(first + i * rows, rows)], land_ref.at[pl.ds(i * rows, rows)], sems.at[i]
        )
        for i in range(chunks)
    ]
    for copy in copies:
        copy.start()

    def finish():
        for i, copy in enumerate(copies):
            copy.wait()
            part = slice(i * rows, (i + 1) * rows)
            high_ref[:, part], low_ref[:, part] = high_and_low(land_ref[part, :].T)

    return finish


def in_hbm(x):
    return pltpu.with_memory_space_constraint(x, pltpu.HBM)


def stage_kernel(
    pair_ref, tile_hbm, tasks_hbm, virt_hbm, amps_hbm, ints_hbm,
    facts_ref, denom_ref, own_ref, high_ref, low_ref,
    tile_ref, tasks_ref, virt_ref, sems, land_ref, ints_sems,
):
    copies = [
        pltpu.make_async_copy(src, dst, sems.at[i])
        for i, (src, dst) in enumerate(
            [
                (tile_hbm, tile_ref),
                (tasks_hbm, tasks_ref),
                (virt_hbm, virt_ref),
                (amps_hbm, own_ref),
            ]
        )
    ]
    for copy in copies:
        copy.start()
    finish = split_rows(ints_hbm, 0, land_ref, ints_sems, high_ref, low_ref)
    my_node, my_dev = lax.axis_index("node"), lax.axis_index("dev")
    nodes = tasks_ref.shape[0]
    for copy in copies:
        copy.wait()
    row = tile_ref[pl.ds(my_node, 1), :]
    position = lax.broadcasted_iota(jnp.int32, row.shape, 1)
    for core in range(2):
        owner = my_dev // 2 * 2 + core
        slot = jnp.sum(jnp.where(row == owner, position, 0), axis=1, keepdims=True)
        facts_ref[core : core + 1, :] = jnp.broadcast_to(slot, (1, LANES))
    for k in range(nodes):
        task = tasks_ref[my_node ^ k]
        hit = jnp.where((task[0:1] == my_node) & (task[1:2] == my_dev), 1, 0)
        hit = jnp.max(hit, axis=1, keepdims=True)
        facts_ref[HITS + k : HITS + k + 1, :] = jnp.broadcast_to(hit, (1, LANES))
    denom = pair_ref[...] - virt_ref[...]
    for j in range(denom_ref.shape[1]):
        denom_ref[:, j, :] = denom[:, j * LANES : (j + 1) * LANES]
    finish()


def split_kernel(after_ref, ints_hbm, high_ref, low_ref, land_ref, sems):
    del after_ref
    split_rows(ints_hbm, ints_hbm.shape[0] - high_ref.shape[1], land_ref, sems, high_ref, low_ref)()


def pick_kernel(facts_ref, own_ref, *refs):
    pieces, held_ref = refs[:-1], refs[-1]
    my_dev = lax.axis_index("dev")
    steps = [
        jnp.where(my_dev % 2 == 0, odd, even) for even, odd in gather_steps(2 * len(pieces) + 2)
    ]
    for core in range(2):
        wanted = (facts_ref[core : core + 1, 0:1] // 2) ^ (my_dev // 2)
        tile = own_ref[...]
        for step, piece in zip(steps, pieces):
            tile = jnp.where(wanted == step, piece[...], tile)
        held_ref[core] = tile


def merge_kernel(facts_ref, held_ref, got_ref, both_ref, mine_ref, theirs_ref):
    my_dev = lax.axis_index("dev")
    my_core = my_dev % 2
    for core in range(2):
        slot = facts_ref[core : core + 1, 0:1]
        here = (slot % 2 == my_core) == (slot // 2 == my_dev // 2)
        both_ref[core] = jnp.where(here, held_ref[core], got_ref[core])
    mine_ref[...] = both_ref[my_core]
    theirs_ref[...] = both_ref[1 - my_core]


def theirs_kernel(after_ref, both_ref, theirs_ref):
    del after_ref
    theirs_ref[...] = both_ref[1 - lax.axis_index("dev") % 2]


def product_kernel(facts_ref, high_a_ref, low_a_ref, high_b_ref, low_b_ref, mine_ref, last_ref, *refs):
    fetched, handed = refs[: len(refs) // 2 - 1], refs[len(refs) // 2 - 1 : -2]
    out_ref, rows_ref = refs[-2:]
    my_node, my_core = lax.axis_index("node"), lax.axis_index("dev") % 2
    pairs = mine_ref.shape[0]
    total = rows_ref.shape[0]

    def place(k, tile):
        start = pl.multiple_of((my_node ^ k) * pairs, pairs)
        hit = facts_ref[pl.ds(HITS + k, 1), 0:1]
        rows_ref[pl.ds(start, pairs), :] = jnp.where(hit > 0, tile, 0.0)

    place(0, mine_ref[...])
    place(2 * len(fetched) + 1, last_ref[...])
    for i, (fetched_ref, handed_ref) in enumerate(zip(fetched, handed)):
        place(2 * i + 1 + my_core, fetched_ref[my_core])
        place(2 * i + 2 - my_core, handed_ref[...])
    amp_high, amp_low = high_and_low(rows_ref[...])
    amp_both = jnp.concatenate([amp_high, amp_low], axis=0)
    first = 0
    for high_ref, low_ref in ((high_a_ref, low_a_ref), (high_b_ref, low_b_ref)):
        both = jnp.dot(amp_both, high_ref[...], preferred_element_type=jnp.float32)
        rest = jnp.dot(amp_high, low_ref[...], preferred_element_type=jnp.float32)
        result = both[:total] + (both[total:] + rest)
        for position, row in enumerate(exchange_order(total)):
            for j in range(high_ref.shape[1] // LANES):
                out_ref[position, first + j, :] = result[row, j * LANES : (j + 1) * LANES]
        first += high_ref.shape[1] // LANES


def resid_kernel(devs, terms_ref, denom_ref, resid_ref):
    sums = [None] * resid_ref.shape[0]
    for position, device in enumerate(exchange_order(terms_ref.shape[0])):
        node, term = device // devs, terms_ref[position]
        sums[node] = term if sums[node] is None else sums[node] + term
    for node, total in enumerate(sums):
        resid_ref[node] = total / denom_ref[node]


def on_device(amps, amp_tile, ints, tasks, pair_energy, virt_energy):
    nodes, devs = lax.axis_size("node"), lax.axis_size("dev")
    pairs, width = amps.shape[2], amps.shape[3]
    groups = width // LANES
    tile = jax.ShapeDtypeStruct((pairs, width), jnp.float32)
    task_rows = jnp.swapaxes(tasks, 1, 2)

    own = amps[0, 0]
    others = [
        lax.ppermute(own, "dev", [(i, i ^ (2 * steps[i % 2] + 1)) for i in range(devs)])
        for steps in gather_steps(devs)
    ]
    chunk = width // 4

    def part(chunks):
        return jax.ShapeDtypeStruct((width, chunks * chunk), jnp.bfloat16), [
            pltpu.VMEM((chunks * chunk, width), jnp.float32),
            pltpu.SemaphoreType.DMA((chunks,)),
        ]

    early, early_landing = part(1)
    late, late_landing = part(3)
    facts, denom, own, high_a, low_a = call(
        stage_kernel,
        "stage",
        (
            jax.ShapeDtypeStruct((HITS + nodes, LANES), jnp.int32),
            jax.ShapeDtypeStruct((nodes, groups, LANES), jnp.float32),
            tile,
            early,
            early,
        ),
        [VMEM] + [HBM] * 5,
        [
            pltpu.VMEM(amp_tile.shape, jnp.int32),
            pltpu.VMEM(task_rows.shape, jnp.int32),
            pltpu.VMEM(virt_energy.shape, jnp.float32),
            pltpu.SemaphoreType.DMA((4,)),
            *early_landing,
        ],
        flops=width * width,
        moved=4 * width * width,
    )(pair_energy, *map(in_hbm, (amp_tile, task_rows, virt_energy, own, ints[0, 0])))
    both = jax.ShapeDtypeStruct((2, pairs, width), jnp.float32)
    swap = [(i, i ^ 1) for i in range(devs)]
    held = call(pick_kernel, "pick", both, [VMEM] * (2 + len(others)))(facts, own, *others)
    got = lax.ppermute(held, "dev", swap)
    chip_tiles, mine, theirs = call(merge_kernel, "merge", (both, tile, tile), [VMEM] * 3)(facts, held, got)

    fetched = [
        lax.ppermute(
            chip_tiles,
            ("node", "dev"),
            [
                (n * devs + d, (n ^ (k + d % 2)) * devs + d)
                for n in range(nodes)
                for d in range(devs)
            ],
        )
        for k in range(1, nodes - 1, 2)
    ]
    last = lax.ppermute(
        theirs,
        ("node", "dev"),
        [
            (n * devs + d, (n ^ (nodes - 1)) * devs + (d ^ 1))
            for n in range(nodes)
            for d in range(devs)
        ],
    )
    high_b, low_b = call(
        split_kernel,
        "split",
        (late, late),
        [VMEM, HBM],
        late_landing,
        flops=width * width,
        moved=4 * width * width,
    )(mine, in_hbm(ints[0, 0]))
    handed = [
        lax.ppermute(call(theirs_kernel, "theirs", tile, [VMEM] * 2)(high_b, tiles), "dev", swap)
        for tiles in fetched
    ]
    products = call(
        product_kernel,
        "product",
        jax.ShapeDtypeStruct((nodes * pairs, groups, LANES), jnp.float32),
        [VMEM] * (7 + 2 * len(fetched)),
        [pltpu.VMEM((nodes * pairs, width), jnp.float32)],
        flops=6 * nodes * pairs * width * width,
        moved=4 * width * width,
    )(facts, high_a, low_a, high_b, low_b, mine, last, *fetched, *handed)

    terms = lax.all_to_all(
        products,
        ("node", "dev"),
        0,
        0,
        tiled=True,
        axis_index_groups=[exchange_order(nodes * devs)],
    )
    resid = call(
        functools.partial(resid_kernel, devs),
        "resid",
        jax.ShapeDtypeStruct((nodes, groups, LANES), jnp.float32),
        [VMEM] * 2,
    )(terms, denom)
    return resid.reshape(1, 1, nodes * width)


def solution(mesh):
    in_specs = (
        P("node", "dev", None, None),
        P(),
        P("node", "dev", None, None),
        P(),
        P("node", "dev"),
        P(),
    )
    return jax.shard_map(
        on_device, mesh=mesh, in_specs=in_specs, out_specs=P("node", "dev", None), check_vma=False
    )
```

```python
import functools
import math

import jax
import jax.numpy as jnp
from jax import lax
from jax.experimental import pallas as pl
from jax.experimental.pallas import tpu as pltpu
from jax.sharding import PartitionSpec as P

LANES = 128
VMEM_LIMIT = 24 * 2**20
HITS = 2
VMEM = pl.BlockSpec(memory_space=pltpu.VMEM)
HBM = pl.BlockSpec(memory_space=pltpu.HBM)


def exchange_order(total):
    step = total - 5 if math.gcd(5, total) == 1 else 1
    return [(j * step) % total for j in range(total)]


def gather_steps(devs):
    odd = list(range(1, devs // 2))
    even = odd[1::-1] + odd[2:]
    return list(zip(even, odd))


def call(kernel, name, out_shape, in_specs, scratch=(), flops=0, moved=0):
    return pl.pallas_call(
        kernel,
        out_shape=out_shape,
        in_specs=in_specs,
        out_specs=jax.tree.map(lambda _: VMEM, out_shape),
        scratch_shapes=list(scratch),
        compiler_params=pltpu.CompilerParams(vmem_limit_bytes=VMEM_LIMIT),
        cost_estimate=pl.CostEstimate(flops=flops, bytes_accessed=moved, transcendentals=0),
        name=name,
    )


def high_and_low(x):
    high = x.astype(jnp.bfloat16)
    return high, (x - high.astype(jnp.float32)).astype(jnp.bfloat16)


def split_rows(ints_hbm, first, land_ref, sems, high_ref, low_ref):
    chunks = sems.shape[0]
    rows = high_ref.shape[1] // chunks
    copies = [
        pltpu.make_async_copy(
            ints_hbm.at[pl.ds(first + i * rows, rows)], land_ref.at[pl.ds(i * rows, rows)], sems.at[i]
        )
        for i in range(chunks)
    ]
    for copy in copies:
        copy.start(priority=1)

    def finish():
        for i, copy in enumerate(copies):
            copy.wait()
            part = slice(i * rows, (i + 1) * rows)
            high_ref[:, part], low_ref[:, part] = high_and_low(land_ref[part, :].T)

    return finish


def in_hbm(x):
    return pltpu.with_memory_space_constraint(x, pltpu.HBM)


def stage_kernel(
    pair_ref, tile_hbm, tasks_hbm, virt_hbm, amps_hbm, ints_hbm,
    facts_ref, denom_ref, own_ref, high_ref, low_ref,
    tile_ref, tasks_ref, virt_ref, sems, land_ref, ints_sems,
):
    copies = [
        pltpu.make_async_copy(src, dst, sems.at[i])
        for i, (src, dst) in enumerate(
            [
                (tile_hbm, tile_ref),
                (tasks_hbm, tasks_ref),
                (virt_hbm, virt_ref),
                (amps_hbm, own_ref),
            ]
        )
    ]
    for copy in copies:
        copy.start()
    finish = split_rows(ints_hbm, 0, land_ref, ints_sems, high_ref, low_ref)
    my_node, my_dev = lax.axis_index("node"), lax.axis_index("dev")
    nodes = tasks_ref.shape[0]
    for copy in copies:
        copy.wait()
    row = tile_ref[pl.ds(my_node, 1), :]
    position = lax.broadcasted_iota(jnp.int32, row.shape, 1)
    for core in range(2):
        owner = my_dev // 2 * 2 + core
        slot = jnp.sum(jnp.where(row == owner, position, 0), axis=1, keepdims=True)
        facts_ref[core : core + 1, :] = jnp.broadcast_to(slot, (1, LANES))
    for k in range(nodes):
        task = tasks_ref[my_node ^ k]
        hit = jnp.where((task[0:1] == my_node) & (task[1:2] == my_dev), 1, 0)
        hit = jnp.max(hit, axis=1, keepdims=True)
        facts_ref[HITS + k : HITS + k + 1, :] = jnp.broadcast_to(hit, (1, LANES))
    denom = pair_ref[0, 0] - virt_ref[...]
    for j in range(denom_ref.shape[1]):
        denom_ref[:, j, :] = denom[:, j * LANES : (j + 1) * LANES]
    finish()


def split_kernel(after_ref, ints_hbm, high_ref, low_ref, land_ref, sems):
    del after_ref
    split_rows(ints_hbm, ints_hbm.shape[0] - high_ref.shape[1], land_ref, sems, high_ref, low_ref)()


def pick_kernel(facts_ref, own_ref, *refs):
    pieces, held_ref = refs[:-1], refs[-1]
    my_dev = lax.axis_index("dev")
    steps = [
        jnp.where(my_dev % 2 == 0, odd, even) for even, odd in gather_steps(2 * len(pieces) + 2)
    ]
    for core in range(2):
        wanted = (facts_ref[core : core + 1, 0:1] // 2) ^ (my_dev // 2)
        tile = own_ref[...]
        for step, piece in zip(steps, pieces):
            tile = jnp.where(wanted == step, piece[...], tile)
        held_ref[core] = tile


def merge_kernel(facts_ref, held_ref, got_ref, both_ref, mine_ref, theirs_ref):
    my_dev = lax.axis_index("dev")
    my_core = my_dev % 2
    for core in range(2):
        slot = facts_ref[core : core + 1, 0:1]
        here = (slot % 2 == my_core) == (slot // 2 == my_dev // 2)
        both_ref[core] = jnp.where(here, held_ref[core], got_ref[core])
    mine_ref[...] = both_ref[my_core]
    theirs_ref[...] = both_ref[1 - my_core]


def theirs_kernel(after_ref, both_ref, theirs_ref):
    del after_ref
    theirs_ref[...] = both_ref[1 - lax.axis_index("dev") % 2]


def product_kernel(facts_ref, high_a_ref, low_a_ref, high_b_ref, low_b_ref, mine_ref, last_ref, *refs):
    fetched, handed = refs[: len(refs) // 2 - 1], refs[len(refs) // 2 - 1 : -2]
    out_ref, rows_ref = refs[-2:]
    my_node, my_core = lax.axis_index("node"), lax.axis_index("dev") % 2
    pairs = mine_ref.shape[0]
    total = rows_ref.shape[0]

    def place(k, tile):
        start = pl.multiple_of((my_node ^ k) * pairs, pairs)
        hit = facts_ref[pl.ds(HITS + k, 1), 0:1]
        rows_ref[pl.ds(start, pairs), :] = jnp.where(hit > 0, tile, 0.0)

    place(0, mine_ref[...])
    place(2 * len(fetched) + 1, last_ref[...])
    for i, (fetched_ref, handed_ref) in enumerate(zip(fetched, handed)):
        place(2 * i + 1 + my_core, fetched_ref[my_core])
        place(2 * i + 2 - my_core, handed_ref[...])
    amp_high, amp_low = high_and_low(rows_ref[...])
    amp_both = jnp.concatenate([amp_high, amp_low], axis=0)
    first = 0
    for high_ref, low_ref in ((high_a_ref, low_a_ref), (high_b_ref, low_b_ref)):
        both = jnp.dot(amp_both, high_ref[...], preferred_element_type=jnp.float32)
        rest = jnp.dot(amp_high, low_ref[...], preferred_element_type=jnp.float32)
        result = both[:total] + (both[total:] + rest)
        for position, row in enumerate(exchange_order(total)):
            for j in range(high_ref.shape[1] // LANES):
                out_ref[position, first + j, :] = result[row, j * LANES : (j + 1) * LANES]
        first += high_ref.shape[1] // LANES


def resid_kernel(devs, terms_ref, denom_ref, resid_ref):
    sums = [None] * resid_ref.shape[0]
    for position, device in enumerate(exchange_order(terms_ref.shape[0])):
        node, term = device // devs, terms_ref[position]
        sums[node] = term if sums[node] is None else sums[node] + term
    for node, total in enumerate(sums):
        resid_ref[node] = total / denom_ref[node]


def on_device(amps, amp_tile, ints, tasks, pair_energy, virt_energy):
    nodes, devs = lax.axis_size("node"), lax.axis_size("dev")
    pairs, width = amps.shape[2], amps.shape[3]
    groups = width // LANES
    tile = jax.ShapeDtypeStruct((pairs, width), jnp.float32)
    task_rows = jnp.swapaxes(tasks, 1, 2)

    own = amps[0, 0]
    others = [
        lax.ppermute(own, "dev", [(i, i ^ (2 * steps[i % 2] + 1)) for i in range(devs)])
        for steps in gather_steps(devs)
    ]
    chunk = width // 4

    def part(chunks):
        return jax.ShapeDtypeStruct((width, chunks * chunk), jnp.bfloat16), [
            pltpu.VMEM((chunks * chunk, width), jnp.float32),
            pltpu.SemaphoreType.DMA((chunks,)),
        ]

    early, early_landing = part(1)
    late, late_landing = part(3)
    facts, denom, own, high_a, low_a = call(
        stage_kernel,
        "stage",
        (
            jax.ShapeDtypeStruct((HITS + nodes, LANES), jnp.int32),
            jax.ShapeDtypeStruct((nodes, groups, LANES), jnp.float32),
            tile,
            early,
            early,
        ),
        [pl.BlockSpec(memory_space=pltpu.SMEM)] + [HBM] * 5,
        [
            pltpu.VMEM(amp_tile.shape, jnp.int32),
            pltpu.VMEM(task_rows.shape, jnp.int32),
            pltpu.VMEM(virt_energy.shape, jnp.float32),
            pltpu.SemaphoreType.DMA((4,)),
            *early_landing,
        ],
        flops=width * width,
        moved=4 * width * width,
    )(pair_energy, *map(in_hbm, (amp_tile, task_rows, virt_energy, own, ints[0, 0])))
    both = jax.ShapeDtypeStruct((2, pairs, width), jnp.float32)
    swap = [(i, i ^ 1) for i in range(devs)]
    held = call(pick_kernel, "pick", both, [VMEM] * (2 + len(others)))(facts, own, *others)
    got = lax.ppermute(held, "dev", swap)
    chip_tiles, mine, theirs = call(merge_kernel, "merge", (both, tile, tile), [VMEM] * 3)(facts, held, got)

    fetched = [
        lax.ppermute(
            chip_tiles,
            ("node", "dev"),
            [
                (n * devs + d, (n ^ (k + d % 2)) * devs + d)
                for n in range(nodes)
                for d in range(devs)
            ],
        )
        for k in range(1, nodes - 1, 2)
    ]
    last = lax.ppermute(
        theirs,
        ("node", "dev"),
        [
            (n * devs + d, (n ^ (nodes - 1)) * devs + (d ^ 1))
            for n in range(nodes)
            for d in range(devs)
        ],
    )
    high_b, low_b = call(
        split_kernel,
        "split",
        (late, late),
        [VMEM, HBM],
        late_landing,
        flops=width * width,
        moved=4 * width * width,
    )(mine, in_hbm(ints[0, 0]))
    handed = [
        lax.ppermute(call(theirs_kernel, "theirs", tile, [VMEM] * 2)(high_b, tiles), "dev", swap)
        for tiles in fetched
    ]
    products = call(
        product_kernel,
        "product",
        jax.ShapeDtypeStruct((nodes * pairs, groups, LANES), jnp.float32),
        [VMEM] * (7 + 2 * len(fetched)),
        [pltpu.VMEM((nodes * pairs, width), jnp.float32)],
        flops=6 * nodes * pairs * width * width,
        moved=4 * width * width,
    )(facts, high_a, low_a, high_b, low_b, mine, last, *fetched, *handed)

    terms = lax.all_to_all(
        products,
        ("node", "dev"),
        0,
        0,
        tiled=True,
        axis_index_groups=[exchange_order(nodes * devs)],
    )
    resid = call(
        functools.partial(resid_kernel, devs),
        "resid",
        jax.ShapeDtypeStruct((nodes, groups, LANES), jnp.float32),
        [VMEM] * 2,
    )(terms, denom)
    return resid.reshape(1, 1, nodes * width)


def solution(mesh):
    in_specs = (
        P("node", "dev", None, None),
        P(),
        P("node", "dev", None, None),
        P(),
        P("node", "dev"),
        P(),
    )
    return jax.shard_map(
        on_device, mesh=mesh, in_specs=in_specs, out_specs=P("node", "dev", None), check_vma=False
    )
```

```python
import functools
import math

import jax
import jax.numpy as jnp
from jax import lax
from jax.experimental import pallas as pl
from jax.experimental.pallas import tpu as pltpu
from jax.sharding import PartitionSpec as P

LANES = 128
VMEM_LIMIT = 24 * 2**20
HITS = 2
VMEM = pl.BlockSpec(memory_space=pltpu.VMEM)
HBM = pl.BlockSpec(memory_space=pltpu.HBM)


def exchange_order(total):
    step = total - 5 if math.gcd(5, total) == 1 else 1
    return [(j * step) % total for j in range(total)]


def gather_steps(devs):
    odd = list(range(1, devs // 2))
    even = odd[1::-1] + odd[2:]
    return list(zip(even, odd))


def call(kernel, name, out_shape, in_specs, scratch=(), flops=0, moved=0):
    return pl.pallas_call(
        kernel,
        out_shape=out_shape,
        in_specs=in_specs,
        out_specs=jax.tree.map(lambda _: VMEM, out_shape),
        scratch_shapes=list(scratch),
        compiler_params=pltpu.CompilerParams(vmem_limit_bytes=VMEM_LIMIT),
        cost_estimate=pl.CostEstimate(flops=flops, bytes_accessed=moved, transcendentals=0),
        name=name,
    )


def high_and_low(x):
    high = x.astype(jnp.bfloat16)
    return high, (x - high.astype(jnp.float32)).astype(jnp.bfloat16)


def split_rows(ints_hbm, first, land_ref, sems, high_ref, low_ref):
    chunks = sems.shape[0]
    rows = high_ref.shape[1] // chunks
    copies = [
        pltpu.make_async_copy(
            ints_hbm.at[pl.ds(first + i * rows, rows)], land_ref.at[pl.ds(i * rows, rows)], sems.at[i]
        )
        for i in range(chunks)
    ]
    for copy in copies:
        copy.start(priority=1)

    def finish():
        for i, copy in enumerate(copies):
            copy.wait()
            part = slice(i * rows, (i + 1) * rows)
            high_ref[:, part], low_ref[:, part] = high_and_low(land_ref[part, :].T)

    return finish


def in_hbm(x):
    return pltpu.with_memory_space_constraint(x, pltpu.HBM)


def stage_kernel(
    pair_ref, tile_hbm, tasks_hbm, virt_hbm, amps_hbm, ints_hbm,
    facts_ref, denom_ref, own_ref, high_ref, low_ref,
    tile_ref, tasks_ref, virt_ref, sems, land_ref, ints_sems,
):
    copies = [
        pltpu.make_async_copy(src, dst, sems.at[i])
        for i, (src, dst) in enumerate(
            [
                (tile_hbm, tile_ref),
                (tasks_hbm, tasks_ref),
                (virt_hbm, virt_ref),
                (amps_hbm, own_ref),
            ]
        )
    ]
    for copy in copies:
        copy.start()
    finish = split_rows(ints_hbm, 0, land_ref, ints_sems, high_ref, low_ref)
    my_node, my_dev = lax.axis_index("node"), lax.axis_index("dev")
    nodes = tasks_ref.shape[0]
    for copy in copies:
        copy.wait()
    row = tile_ref[pl.ds(my_node, 1), :]
    position = lax.broadcasted_iota(jnp.int32, row.shape, 1)
    for core in range(2):
        owner = my_dev // 2 * 2 + core
        slot = jnp.sum(jnp.where(row == owner, position, 0), axis=1, keepdims=True)
        facts_ref[core : core + 1, :] = jnp.broadcast_to(slot, (1, LANES))
    for k in range(nodes):
        task = tasks_ref[my_node ^ k]
        hit = jnp.where((task[0:1] == my_node) & (task[1:2] == my_dev), 1, 0)
        hit = jnp.max(hit, axis=1, keepdims=True)
        facts_ref[HITS + k : HITS + k + 1, :] = jnp.broadcast_to(hit, (1, LANES))
    denom = pair_ref[...] - virt_ref[...]
    for j in range(denom_ref.shape[1]):
        denom_ref[:, j, :] = denom[:, j * LANES : (j + 1) * LANES]
    finish()


def split_kernel(after_ref, ints_hbm, high_ref, low_ref, land_ref, sems):
    del after_ref
    split_rows(ints_hbm, ints_hbm.shape[0] - high_ref.shape[1], land_ref, sems, high_ref, low_ref)()


def pick_kernel(facts_ref, own_ref, *refs):
    pieces, held_ref = refs[:-1], refs[-1]
    my_dev = lax.axis_index("dev")
    steps = [
        jnp.where(my_dev % 2 == 0, odd, even) for even, odd in gather_steps(2 * len(pieces) + 2)
    ]
    for core in range(2):
        wanted = (facts_ref[core : core + 1, 0:1] // 2) ^ (my_dev // 2)
        tile = own_ref[...]
        for step, piece in zip(steps, pieces):
            tile = jnp.where(wanted == step, piece[...], tile)
        held_ref[core] = tile


def merge_kernel(facts_ref, held_ref, got_ref, both_ref, mine_ref, theirs_ref):
    my_dev = lax.axis_index("dev")
    my_core = my_dev % 2
    for core in range(2):
        slot = facts_ref[core : core + 1, 0:1]
        here = (slot % 2 == my_core) == (slot // 2 == my_dev // 2)
        both_ref[core] = jnp.where(here, held_ref[core], got_ref[core])
    mine_ref[...] = both_ref[my_core]
    theirs_ref[...] = both_ref[1 - my_core]


def theirs_kernel(after_ref, both_ref, theirs_ref):
    del after_ref
    theirs_ref[...] = both_ref[1 - lax.axis_index("dev") % 2]


def product_kernel(facts_ref, high_a_ref, low_a_ref, high_b_ref, low_b_ref, mine_ref, last_ref, *refs):
    fetched, handed = refs[: len(refs) // 2 - 1], refs[len(refs) // 2 - 1 : -2]
    out_ref, rows_ref = refs[-2:]
    my_node, my_core = lax.axis_index("node"), lax.axis_index("dev") % 2
    pairs = mine_ref.shape[0]
    total = rows_ref.shape[0]

    def place(k, tile):
        start = pl.multiple_of((my_node ^ k) * pairs, pairs)
        hit = facts_ref[pl.ds(HITS + k, 1), 0:1]
        rows_ref[pl.ds(start, pairs), :] = jnp.where(hit > 0, tile, 0.0)

    place(0, mine_ref[...])
    place(2 * len(fetched) + 1, last_ref[...])
    for i, (fetched_ref, handed_ref) in enumerate(zip(fetched, handed)):
        place(2 * i + 1 + my_core, fetched_ref[my_core])
        place(2 * i + 2 - my_core, handed_ref[...])
    amp_high, amp_low = high_and_low(rows_ref[...])
    amp_both = jnp.concatenate([amp_high, amp_low], axis=0)
    first = 0
    for high_ref, low_ref in ((high_a_ref, low_a_ref), (high_b_ref, low_b_ref)):
        both = jnp.dot(amp_both, high_ref[...], preferred_element_type=jnp.float32)
        rest = jnp.dot(amp_high, low_ref[...], preferred_element_type=jnp.float32)
        result = both[:total] + (both[total:] + rest)
        for position, row in enumerate(exchange_order(total)):
            for j in range(high_ref.shape[1] // LANES):
                out_ref[position, first + j, :] = result[row, j * LANES : (j + 1) * LANES]
        first += high_ref.shape[1] // LANES


def resid_kernel(devs, terms_ref, denom_ref, resid_ref):
    sums = [None] * resid_ref.shape[0]
    for position, device in enumerate(exchange_order(terms_ref.shape[0])):
        node, term = device // devs, terms_ref[position]
        sums[node] = term if sums[node] is None else sums[node] + term
    for node, total in enumerate(sums):
        resid_ref[node] = total / denom_ref[node]


def on_device(amps, amp_tile, ints, tasks, pair_energy, virt_energy):
    nodes, devs = lax.axis_size("node"), lax.axis_size("dev")
    pairs, width = amps.shape[2], amps.shape[3]
    groups = width // LANES
    tile = jax.ShapeDtypeStruct((pairs, width), jnp.float32)
    task_rows = jnp.swapaxes(tasks, 1, 2)

    own = amps[0, 0]
    others = [
        lax.ppermute(own, "dev", [(i, i ^ (2 * steps[i % 2] + 1)) for i in range(devs)])
        for steps in gather_steps(devs)
    ]
    chunk = width // 4

    def part(chunks):
        return jax.ShapeDtypeStruct((width, chunks * chunk), jnp.bfloat16), [
            pltpu.VMEM((chunks * chunk, width), jnp.float32),
            pltpu.SemaphoreType.DMA((chunks,)),
        ]

    early, early_landing = part(1)
    late, late_landing = part(3)
    facts, denom, own, high_a, low_a = call(
        stage_kernel,
        "stage",
        (
            jax.ShapeDtypeStruct((HITS + nodes, LANES), jnp.int32),
            jax.ShapeDtypeStruct((nodes, groups, LANES), jnp.float32),
            tile,
            early,
            early,
        ),
        [VMEM] + [HBM] * 5,
        [
            pltpu.VMEM(amp_tile.shape, jnp.int32),
            pltpu.VMEM(task_rows.shape, jnp.int32),
            pltpu.VMEM(virt_energy.shape, jnp.float32),
            pltpu.SemaphoreType.DMA((4,)),
            *early_landing,
        ],
        flops=width * width,
        moved=4 * width * width,
    )(pair_energy, *map(in_hbm, (amp_tile, task_rows, virt_energy, own, ints[0, 0])))
    both = jax.ShapeDtypeStruct((2, pairs, width), jnp.float32)
    swap = [(i, i ^ 1) for i in range(devs)]
    held = call(pick_kernel, "pick", both, [VMEM] * (2 + len(others)))(facts, own, *others)
    got = lax.ppermute(held, "dev", swap)
    chip_tiles, mine, theirs = call(merge_kernel, "merge", (both, tile, tile), [VMEM] * 3)(facts, held, got)

    fetched = [
        lax.ppermute(
            chip_tiles,
            ("node", "dev"),
            [
                (n * devs + d, (n ^ (k + d % 2)) * devs + d)
                for n in range(nodes)
                for d in range(devs)
            ],
        )
        for k in range(1, nodes - 1, 2)
    ]
    last = lax.ppermute(
        theirs,
        ("node", "dev"),
        [
            (n * devs + d, (n ^ (nodes - 1)) * devs + (d ^ 1))
            for n in range(nodes)
            for d in range(devs)
        ],
    )
    high_b, low_b = call(
        split_kernel,
        "split",
        (late, late),
        [VMEM, HBM],
        late_landing,
        flops=width * width,
        moved=4 * width * width,
    )(mine, in_hbm(ints[0, 0]))
    handed = [
        lax.ppermute(call(theirs_kernel, "theirs", tile, [VMEM] * 2)(high_b, tiles), "dev", swap)
        for tiles in fetched
    ]
    products = call(
        product_kernel,
        "product",
        jax.ShapeDtypeStruct((nodes * pairs, groups, LANES), jnp.float32),
        [VMEM] * (7 + 2 * len(fetched)),
        [pltpu.VMEM((nodes * pairs, width), jnp.float32)],
        flops=6 * nodes * pairs * width * width,
        moved=4 * width * width,
    )(facts, high_a, low_a, high_b, low_b, mine, last, *fetched, *handed)

    terms = lax.all_to_all(
        products,
        ("node", "dev"),
        0,
        0,
        tiled=True,
        axis_index_groups=[exchange_order(nodes * devs)],
    )
    resid = call(
        functools.partial(resid_kernel, devs),
        "resid",
        jax.ShapeDtypeStruct((nodes, groups, LANES), jnp.float32),
        [VMEM] * 2,
    )(terms, denom)
    return resid.reshape(1, 1, nodes * width)


def solution(mesh):
    in_specs = (
        P("node", "dev", None, None),
        P(),
        P("node", "dev", None, None),
        P(),
        P("node", "dev"),
        P(),
    )
    return jax.shard_map(
        on_device, mesh=mesh, in_specs=in_specs, out_specs=P("node", "dev", None), check_vma=False
    )
```
